128 devices in a mesh: ka: 8 (over z, x_hi), chol: 2 (over core), orb: 8 (over x_lo, y).
Axes of the slice: x: 4 (x_hi: 2, x_lo: 2; x = x_hi * 2 + x_lo), y: 4, z: 4, core: 2. Of those that a mesh axis runs over, the one named last changes fastest.
Arguments:
- chol_pairs: bfloat16 [2, 8, 2, 800, 104, 104], P(None, 'ka', None, 'chol', 'orb'), may hold values from -0.23925781 to 0.23925781
- green: bfloat16 [8, 4, 2, 104, 104], P('ka', None, None, 'orb'), may hold values from -0.625 to 0.625
- screening: float32 [2, 4, 800], P(None, None, 'chol'), may hold values from 0.25 to 4
Outputs:
- self_energy: float32 [8, 4, 2, 104, 104], P('ka', None, None, 'orb')
The draws below stay inside these ranges and needn't reach their ends.
All inputs are finite; a program needn't handle non-finite values.
Results may differ from the reference program's by a relative error of at most 0.0028.
Values may be sent and summed in bfloat16 or wider, within the bound.
A program may use at most 256 MiB of HBM per device.

```python
import math
import jax
import jax.numpy as jnp
from jax import lax

NORB = 104
NCHOL = 800
TAU = 4
NQ = 2
KPTS = 8
SHIFT_NEAR = 1
SHIFT_FAR = 4


def levels(key, dims, split, smallest, top_value):
    loudness, own = 1.0, jax.random.fold_in(key, 6)
    for position, blocks in split:
        heights = jnp.exp(jax.random.uniform(jax.random.fold_in(own, position), (blocks,), jnp.float32, smallest / len(split), top_value / len(split)))
        loudness = loudness * jnp.repeat(heights, dims[position] // blocks).reshape([-1 if axis == position else 1 for axis in range(len(dims))])
    return loudness


def bell_draw(key, dims, width, most, cuts=(), held_as=jnp.bfloat16):
    entries = jax.random.normal(key, dims, jnp.float32) * width
    if len(cuts) > 0:
        entries = levels(key, dims, cuts, -0.22, 0.18) * entries
    return jnp.clip(entries, min=-most, max=most).astype(held_as)


def setup_inputs(seed: int = 0) -> dict:
    keys = jax.random.split(jax.random.key(seed), 4)
    chol_pairs = bell_draw(keys[0], (NQ, KPTS, 2, NCHOL, NORB, NORB), 0.04, 0.23925781, ((1, 8), (3, 2), (4, 8)))
    green = bell_draw(keys[1], (KPTS, TAU, 2, NORB, NORB), NORB ** -0.5, 0.625, ((0, 8), (3, 8)))
    screening = jnp.clip(jnp.exp(math.log(4.0) - 2.7725887 * jax.random.uniform(keys[2], (NQ, TAU, NCHOL), jnp.float32) ** levels(keys[2], (NQ, TAU, NCHOL), ((2, 2),), -0.2, 0.2)), 0.25, 4.0)
    return dict(chol_pairs=chol_pairs, green=green, screening=screening)


def reference(chol_pairs, green, screening):
    shifts = (SHIFT_NEAR, SHIFT_FAR)
    total = jnp.zeros((KPTS, TAU, 2, NORB, NORB), jnp.float32)
    for shift_index in range(NQ):
        shifted = jnp.roll(green, shifts[shift_index], axis=0)
        factor = screening[shift_index][:, :, None, None]

        def one_point(operands):
            pairs, green_point = operands
            left_real = pairs[0].astype(jnp.float32)
            left_imag = pairs[1].astype(jnp.float32)
            green_real = green_point[:, 0].astype(jnp.float32)
            green_imag = green_point[:, 1].astype(jnp.float32)
            pattern = "qim,tml->tqil"
            real_part = jnp.einsum(pattern, left_real, green_real) - jnp.einsum(pattern, left_imag, green_imag)
            imag_part = jnp.einsum(pattern, left_real, green_imag) + jnp.einsum(pattern, left_imag, green_real)
            image_real = lax.optimization_barrier((real_part * factor).astype(jnp.bfloat16)).astype(jnp.float32)
            image_imag = lax.optimization_barrier((imag_part * factor).astype(jnp.bfloat16)).astype(jnp.float32)
            second = "tqil,qjl->tij"
            sum_real = jnp.einsum(second, image_real, left_real) + jnp.einsum(second, image_imag, left_imag)
            sum_imag = jnp.einsum(second, image_imag, left_real) - jnp.einsum(second, image_real, left_imag)
            return -jnp.stack([sum_real, sum_imag], axis=1)

        total = total + lax.map(one_point, (chol_pairs[shift_index], shifted))
    return total
```

```python
import functools

import jax
import jax.numpy as jnp
from jax import lax
from jax.experimental import pallas as pl
from jax.experimental.pallas import tpu as pltpu
from jax.sharding import PartitionSpec as P

MESH = pl.DeviceIdType.MESH
BF16 = jnp.bfloat16
F32 = jnp.float32

ORB = 8
ROWS = 13
NORB = 104
PADDED = 112
TAUS = 4
VEC = 16
PER_Q = 25
SLOTS = 6
PLANES = 2 * ROWS
KEPT = 22
SPARE = 128 - NORB
PIECES = 5


def pad_lanes(x):
    return jnp.concatenate([x, jnp.zeros((x.shape[0], 128 - x.shape[1]), x.dtype)], axis=1)


def kernel(
    chol_ref, green_ref, screen_ref, out_ref,
    send, recv, extra, flat, image, rhs, weights, perm, total,
    green_in, green_all, half_in, piece, gathered, result, result_in,
    green_send, green_recv, gather_send, gather_recv, swap_send, swap_recv,
    pair_send, pair_recv, half_send, half_recv, piece_send, piece_recv, out_send, out_recv,
):
    k = lax.axis_index("ka")
    core = lax.axis_index("chol")
    me = lax.axis_index("orb")
    shift = 1 + 3 * core
    source_of = lax.rem(k + 8 - shift, 8)
    target_of = lax.rem(k + shift, 8)
    other = 1 - core

    def peer(d):
        dx, dy = d // 4, d % 4
        x = lax.rem(me // 4 + dx, 2)
        y = lax.rem(lax.rem(me, 4) + dy, 4)
        return x * 4 + y

    barrier = pltpu.get_barrier_semaphore()

    def greet(device):
        pl.semaphore_signal(barrier, inc=1, device_id=device, device_id_type=MESH)

    greet((source_of, core, me))
    greet((target_of, core, me))
    greet((k, other, me))
    for d in range(1, ORB):
        greet((k, core, peer(d)))
    pl.semaphore_wait(barrier, ORB + 2)

    shift_copy = pltpu.make_async_remote_copy(
        src_ref=green_ref, dst_ref=green_in, send_sem=green_send, recv_sem=green_recv,
        device_id=(target_of, core, me), device_id_type=MESH)
    shift_copy.start()

    row = lax.broadcasted_iota(jnp.int32, (256, 256), 0)
    col = lax.broadcasted_iota(jnp.int32, (256, 256), 1)
    hit = (lax.div(row, 16) == lax.rem(col, 16)) & (lax.rem(row, 16) == lax.div(col, 16))
    perm[...] = jnp.where(hit, 1.0, 0.0).astype(BF16)
    weights[...] = jnp.zeros_like(weights)
    rhs[...] = jnp.zeros_like(rhs)
    total[...] = jnp.zeros_like(total)

    shift_copy.wait()
    gather_copies = []
    for d in range(1, ORB):
        copy = pltpu.make_async_remote_copy(
            src_ref=green_in, dst_ref=green_all.at[core, me], send_sem=gather_send,
            recv_sem=gather_recv, device_id=(k, core, peer(d)), device_id_type=MESH)
        copy.start()
        gather_copies.append(copy)
    green_all[core, me] = green_in[...]

    lane = lax.broadcasted_iota(jnp.int32, (VEC, 128), 1)

    def fold(group, put):
        q = lax.div(group, PER_Q)
        at = pl.multiple_of(lax.rem(group, PER_Q) * VEC, VEC)

        def plane(f):
            return pad_lanes(chol_ref[q, f // ROWS, f % ROWS, pl.ds(at, VEC), :].astype(F32))

        for e in range(PLANES - KEPT):
            riding = plane(KEPT + e)
            for p in range(PIECES):
                f = PIECES * e + p
                moved = pltpu.roll(riding, (NORB - SPARE * p) % 128, 1)
                put(f, jnp.where(lane < NORB, plane(f), moved).astype(BF16))
        for f in range(PIECES * (PLANES - KEPT), KEPT):
            put(f, plane(f).astype(BF16))

    def fold_send(slot, group, to):
        def put(f, value):
            send[group, f] = value

        fold(group, put)
        pltpu.make_async_remote_copy(
            src_ref=send.at[group], dst_ref=recv.at[slot, me], send_sem=pair_send.at[slot],
            recv_sem=pair_recv.at[slot], device_id=(k, core, to), device_id_type=MESH).start()

    def fold_own(slot, group):
        def put(f, value):
            recv[slot, me, f] = value

        fold(group, put)

    def send_slot(slot, _):
        def send_one(d, _):
            to = peer(d)
            fold_send(slot, to * SLOTS + slot, to)
            return 0

        lax.fori_loop(1, ORB, send_one, 0)
        fold_own(slot, me * SLOTS + slot)
        return 0

    lax.fori_loop(0, SLOTS, send_slot, 0)

    first, second = 2 * core, 6 - 2 * core
    for number, to in ((0, first), (1, second)):
        left_over = ORB * SLOTS + number

        @pl.when(me != to)
        def _(to=to, left_over=left_over):
            fold_send(SLOTS, left_over, to)

        @pl.when(me == to)
        def _(to=to, left_over=left_over):
            fold_own(SLOTS, left_over)

    def wait_bytes(ref, sem):
        pltpu.make_async_copy(ref, ref, sem).wait()

    wait_bytes(green_all.at[core, pl.ds(0, ORB - 1)], gather_recv)
    swap = pltpu.make_async_remote_copy(
        src_ref=green_all.at[core], dst_ref=green_all.at[core], send_sem=swap_send,
        recv_sem=swap_recv, device_id=(k, other, me), device_id_type=MESH)
    swap.start()
    swap.wait()

    for q in range(2):
        for t in range(TAUS):
            parts = []
            for ri in range(2):
                blocks = [green_all[q, o, t, ri].astype(F32) for o in range(ORB)]
                parts.append(pad_lanes(jnp.concatenate(blocks, axis=0)))
            at = t * 256
            real, imag = parts
            weights[q, 0:NORB, at:at + 128] = real.astype(BF16)
            weights[q, 0:NORB, at + 128:at + 256] = imag.astype(BF16)
            weights[q, 128:128 + NORB, at:at + 128] = (-imag).astype(BF16)
            weights[q, 128:128 + NORB, at + 128:at + 256] = real.astype(BF16)

    def work(slot, group):
        q = lax.div(group, PER_Q)
        at = lax.rem(group, PER_Q) * VEC
        wait_bytes(recv.at[slot, pl.ds(0, ORB - 1)], pair_recv.at[slot])
        for o in range(ORB):
            for e in range(PLANES - KEPT):
                value = jnp.zeros((VEC, 128), F32)
                for p in range(PIECES):
                    carrier = recv[slot, o, PIECES * e + p].astype(F32)
                    back = pltpu.roll(carrier, (128 - NORB + SPARE * p) % 128, 1)
                    value = jnp.where(lane >= SPARE * p, back, value) if p else back
                extra[o, e] = value.astype(BF16)

        def plane(j, ri):
            o, r = j // ROWS, j % ROWS
            f = ri * ROWS + r
            return recv[slot, o, f] if f < KEPT else extra[o, f - KEPT]

        for jb in range(PADDED // 16):
            rows = [j for j in range(16 * jb, 16 * jb + 16) if j < NORB]
            both = jnp.concatenate(
                [jnp.concatenate([plane(j, ri) for j in rows], axis=0) for ri in range(2)], axis=1)
            turned = jnp.dot(perm[:, 0:16 * len(rows)], both, preferred_element_type=F32).astype(BF16)
            for v in range(VEC):
                tile = turned[16 * v:16 * v + 16]
                flat[v, 16 * jb:16 * jb + 16, :] = tile
                rhs[16 * jb:16 * jb + 16, 256 * v:256 * v + 256] = tile
                rhs[128 + 16 * jb:144 + 16 * jb, 256 * v:256 * v + 128] = -tile[:, 128:256]
                rhs[128 + 16 * jb:144 + 16 * jb, 256 * v + 128:256 * v + 256] = tile[:, 0:128]

        step = 4
        for v in range(0, VEC, step):
            left = flat[v:v + step].reshape(step * PADDED, 256)
            for t in range(TAUS):
                y = jnp.dot(left, weights[q, :, 256 * t:256 * t + 256], preferred_element_type=F32)
                for i in range(step):
                    scale = screen_ref[q, t, at + v + i]
                    image[PADDED * t:PADDED * t + PADDED, 256 * (v + i):256 * (v + i) + 256] = (
                        y[PADDED * i:PADDED * i + PADDED] * scale).astype(BF16)
        total[...] += lax.dot_general(
            image[...], rhs[...], (((1,), (1,)), ((), ())), preferred_element_type=F32)

    def work_slot(slot, _):
        work(slot, me * SLOTS + slot)
        return 0

    lax.fori_loop(0, SLOTS, work_slot, 0)
    has_more = (me == first) | (me == second)

    @pl.when(has_more)
    def _():
        work(SLOTS, ORB * SLOTS + jnp.where(me == first, 0, 1))

    half = 2 * PADDED
    swap_half = pltpu.make_async_remote_copy(
        src_ref=total.at[pl.ds(pl.multiple_of(other * half, half), half)], dst_ref=half_in,
        send_sem=half_send, recv_sem=half_recv, device_id=(k, other, me), device_id_type=MESH)
    swap_half.start()
    swap_half.wait()
    mine = total[pl.ds(pl.multiple_of(core * half, half), half), :] + half_in[...]
    for o in range(ORB):
        for t in range(2):
            for ri in range(2):
                at = t * PADDED + ROWS * o
                piece[o, t, ri, 0:ROWS] = -mine[at:at + ROWS, 128 * ri:128 * ri + 128]

    def send_piece(d, _):
        to = peer(d)
        pltpu.make_async_remote_copy(
            src_ref=piece.at[to], dst_ref=gathered.at[me], send_sem=piece_send,
            recv_sem=piece_recv, device_id=(k, core, to), device_id_type=MESH).start()
        return 0

    lax.fori_loop(1, ORB, send_piece, 0)
    gathered[me] = piece[me]
    wait_bytes(gathered.at[pl.ds(0, ORB - 1)], piece_recv)
    summed = gathered[0]
    for o in range(1, ORB):
        summed = summed + gathered[o]
    result[...] = summed
    hand_over = pltpu.make_async_remote_copy(
        src_ref=result, dst_ref=result_in, send_sem=out_send, recv_sem=out_recv,
        device_id=(k, other, me), device_id_type=MESH)
    hand_over.start()
    hand_over.wait()
    out_ref[pl.ds(2 * core, 2)] = result[:, :, 0:ROWS, 0:NORB]
    out_ref[pl.ds(2 * other, 2)] = result_in[:, :, 0:ROWS, 0:NORB]

    wait_bytes(green_all.at[core, pl.ds(0, ORB - 1)], gather_send)
    wait_bytes(piece.at[pl.ds(0, ORB - 1)], piece_send)

    def sent_slot(slot, _):
        wait_bytes(recv.at[slot, pl.ds(0, ORB - 1)], pair_send.at[slot])
        return 0

    lax.fori_loop(0, SLOTS, sent_slot, 0)

    @pl.when(has_more)
    def _():
        wait_bytes(recv.at[SLOTS, pl.ds(0, 1)], pair_send.at[SLOTS])

    @pl.when(jnp.logical_not(has_more))
    def _():
        wait_bytes(recv.at[SLOTS, pl.ds(0, 2)], pair_send.at[SLOTS])


def body(chol_pairs, green, screening):
    planes = jnp.transpose(chol_pairs[:, 0], (0, 1, 3, 2, 4))
    dma = pltpu.SemaphoreType.DMA
    out = pl.pallas_call(
        kernel,
        out_shape=jax.ShapeDtypeStruct((TAUS, 2, ROWS, NORB), F32),
        in_specs=[
            pl.BlockSpec(memory_space=pltpu.VMEM),
            pl.BlockSpec(memory_space=pltpu.VMEM),
            pl.BlockSpec(memory_space=pltpu.SMEM),
        ],
        out_specs=pl.BlockSpec(memory_space=pltpu.VMEM),
        scratch_shapes=[
            pltpu.VMEM((ORB * SLOTS + 2, KEPT, VEC, 128), BF16),
            pltpu.VMEM((SLOTS + 1, ORB, KEPT, VEC, 128), BF16),
            pltpu.VMEM((ORB, PLANES - KEPT, VEC, 128), BF16),
            pltpu.VMEM((VEC, PADDED, 256), BF16),
            pltpu.VMEM((TAUS * PADDED, VEC * 256), BF16),
            pltpu.VMEM((256, VEC * 256), BF16),
            pltpu.VMEM((2, 256, TAUS * 256), BF16),
            pltpu.VMEM((256, 256), BF16),
            pltpu.VMEM((TAUS * PADDED, 256), F32),
            pltpu.VMEM((TAUS, 2, ROWS, NORB), BF16),
            pltpu.VMEM((2, ORB, TAUS, 2, ROWS, NORB), BF16),
            pltpu.VMEM((2 * PADDED, 256), F32),
            pltpu.VMEM((ORB, 2, 2, 16, 128), F32),
            pltpu.VMEM((ORB, 2, 2, 16, 128), F32),
            pltpu.VMEM((2, 2, 16, 128), F32),
            pltpu.VMEM((2, 2, 16, 128), F32),
            dma, dma, dma, dma, dma, dma,
            dma((SLOTS + 1,)), dma((SLOTS + 1,)),
            dma, dma, dma, dma, dma, dma,
        ],
        compiler_params=pltpu.CompilerParams(
            collective_id=0, has_side_effects=True, vmem_limit_bytes=56 * 1024 * 1024),
        cost_estimate=pl.CostEstimate(
            flops=7_200_000_000, bytes_accessed=5_400_000, transcendentals=0),
    )(planes, green[0], screening)
    return out[None]


def solution(mesh):
    placed = (
        P(None, "ka", None, "chol", "orb", None),
        P("ka", None, None, "orb", None),
        P(None, None, "chol"),
    )
    return jax.shard_map(
        body,
        mesh=mesh,
        in_specs=placed,
        out_specs=P("ka", None, None, "orb", None),
        check_vma=False,
    )
```

```python
import functools

import jax
import jax.numpy as jnp
from jax import lax
from jax.experimental import pallas as pl
from jax.experimental.pallas import tpu as pltpu
from jax.sharding import PartitionSpec as P

MESH = pl.DeviceIdType.MESH
BF16 = jnp.bfloat16
F32 = jnp.float32

ORB = 8
ROWS = 13
NORB = 104
PADDED = 112
TAUS = 4
VEC = 16
PER_Q = 25
SLOTS = 6
PLANES = 2 * ROWS
KEPT = 22
SPARE = 128 - NORB
PIECES = 5


def pad_lanes(x):
    return jnp.concatenate([x, jnp.zeros((x.shape[0], 128 - x.shape[1]), x.dtype)], axis=1)


def kernel(
    chol_ref, green_ref, screen_ref, out_ref,
    loaded, send, recv, extra, flat, image, rhs, weights, perm, total, mine,
    green_mine, green_all, half_in, piece, gathered, result, result_in,
    load_sem, ready, gather_send, gather_recv, shift_send, shift_recv, swap_send, swap_recv,
    pair_send, pair_recv, half_send, half_recv, piece_send, piece_recv, out_send, out_recv,
):
    k = lax.axis_index("ka")
    core = lax.axis_index("chol")
    me = lax.axis_index("orb")
    other = 1 - core
    first, second = 2 * core, 6 - 2 * core
    has_more = (me == first) | (me == second)
    half = 2 * PADDED

    def peer(d):
        dx, dy = d // 4, d % 4
        x = lax.rem(me // 4 + dx, 2)
        y = lax.rem(lax.rem(me, 4) + dy, 4)
        return x * 4 + y

    def load(q):
        return pltpu.make_async_copy(chol_ref.at[q], loaded.at[q], load_sem.at[q])

    def wait_bytes(ref, sem):
        pltpu.make_async_copy(ref, ref, sem).wait()

    for q in range(2):
        load(q).start()

    barrier = pltpu.get_barrier_semaphore()

    def greet(device):
        pl.semaphore_signal(barrier, inc=1, device_id=device, device_id_type=MESH)

    near_to = (lax.rem(k + 1, 8), core, peer(4))
    near_from = (lax.rem(k + 7, 8), core, peer(4))
    far = (lax.rem(k + 4, 8), core, me)
    for d in range(1, ORB):
        greet((k, 0, peer(d)))

    @pl.when(core == 1)
    def _():
        greet((k, 0, me))
        greet(near_to)
        greet(near_from)
        greet(far)

    row = lax.broadcasted_iota(jnp.int32, (256, 256), 0)
    col = lax.broadcasted_iota(jnp.int32, (256, 256), 1)
    hit = (lax.div(row, 16) == lax.rem(col, 16)) & (lax.rem(row, 16) == lax.div(col, 16))
    perm[...] = jnp.where(hit, 1.0, 0.0).astype(BF16)
    for at in (PADDED, 128 + PADDED):
        rhs[at:at + 16, :] = jnp.zeros((16, VEC * 256), BF16)
    total[...] = jnp.zeros_like(total)
    weights[...] = jnp.zeros_like(weights)

    lane = lax.broadcasted_iota(jnp.int32, (VEC, 128), 1)

    def fold(group, put):
        q = lax.div(group, PER_Q)
        at = pl.multiple_of(lax.rem(group, PER_Q) * VEC, VEC)

        def plane(f):
            return pad_lanes(loaded[q, f // ROWS, f % ROWS, pl.ds(at, VEC), :].astype(F32))

        for e in range(PLANES - KEPT):
            riding = plane(KEPT + e)
            for p in range(PIECES):
                f = PIECES * e + p
                moved = pltpu.roll(riding, (NORB - SPARE * p) % 128, 1)
                put(f, jnp.where(lane < NORB, plane(f), moved).astype(BF16))
        for f in range(PIECES * (PLANES - KEPT), KEPT):
            put(f, plane(f).astype(BF16))

    def fold_to_send(group):
        def put(f, value):
            send[group, f] = value

        fold(group, put)

    def send_pairs(slot, group, to):
        pltpu.make_async_remote_copy(
            src_ref=send.at[group], dst_ref=recv.at[slot, me], send_sem=pair_send.at[slot],
            recv_sem=pair_recv.at[slot], device_id=(k, core, to), device_id_type=MESH).start()

    def fold_own(slot, group):
        def put(f, value):
            recv[slot, me, f] = value

        fold(group, put)

    for q in range(2):
        load(q).wait()

    def fold_first(d, _):
        fold_to_send(peer(d) * SLOTS)
        return 0

    lax.fori_loop(1, ORB, fold_first, 0)

    @pl.when(core == 0)
    def _():
        pl.semaphore_wait(barrier, 2 * ORB - 1)
        pl.semaphore_signal(ready, inc=1, device_id=(k, 1, me), device_id_type=MESH)

    @pl.when(core == 1)
    def _():
        pl.semaphore_wait(ready, 1)
        for d in range(1, ORB):
            pltpu.make_async_remote_copy(
                src_ref=green_ref, dst_ref=green_mine.at[me], send_sem=gather_send,
                recv_sem=gather_recv, device_id=(k, core, peer(d)), device_id_type=MESH).start()

    def send_first(d, _):
        to = peer(d)
        send_pairs(0, to * SLOTS, to)
        return 0

    lax.fori_loop(1, ORB, send_first, 0)
    fold_own(0, me * SLOTS)

    def send_slot(slot, _):
        def send_one(d, _):
            to = peer(d)
            group = to * SLOTS + slot
            fold_to_send(group)
            send_pairs(slot, group, to)
            return 0

        lax.fori_loop(1, ORB, send_one, 0)
        fold_own(slot, me * SLOTS + slot)
        return 0

    lax.fori_loop(1, SLOTS // 2, send_slot, 0)
    for number, to in ((0, first), (1, second)):
        left_over = ORB * SLOTS + number

        @pl.when(me != to)
        def _(to=to, left_over=left_over):
            fold_to_send(left_over)
            send_pairs(SLOTS, left_over, to)

        @pl.when(me == to)
        def _(left_over=left_over):
            fold_own(SLOTS, left_over)

    @pl.when(core == 1)
    def _():
        green_mine[me] = green_ref[...]
        wait_bytes(green_mine.at[pl.ds(0, ORB - 1)], gather_recv)
        pl.semaphore_wait(barrier, 3)
        for q, device in ((0, near_to), (1, far)):
            pltpu.make_async_remote_copy(
                src_ref=green_mine, dst_ref=green_all.at[q], send_sem=shift_send.at[q],
                recv_sem=shift_recv.at[q], device_id=device, device_id_type=MESH).start()

    lax.fori_loop(SLOTS // 2, SLOTS, send_slot, 0)

    hand_green = pltpu.make_async_remote_copy(
        src_ref=green_all, dst_ref=green_all, send_sem=swap_send,
        recv_sem=swap_recv, device_id=(k, 0, me), device_id_type=MESH)

    @pl.when(core == 1)
    def _():
        for q in range(2):
            wait_bytes(green_all.at[q], shift_recv.at[q])
        hand_green.start()

    @pl.when(core == 0)
    def _():
        hand_green.wait_recv()

    for q in range(2):
        for t in range(TAUS):
            parts = []
            for ri in range(2):
                blocks = [green_all[q, o, t, :, ri, :].astype(F32) for o in range(ORB)]
                parts.append(pad_lanes(jnp.concatenate(blocks, axis=0)))
            at = t * 256
            real, imag = parts
            weights[q, 0:NORB, at:at + 128] = real.astype(BF16)
            weights[q, 0:NORB, at + 128:at + 256] = imag.astype(BF16)
            weights[q, 128:128 + NORB, at:at + 128] = (-imag).astype(BF16)
            weights[q, 128:128 + NORB, at + 128:at + 256] = real.astype(BF16)

    swap_half = pltpu.make_async_remote_copy(
        src_ref=total.at[pl.ds(pl.multiple_of(other * half, half), half)], dst_ref=half_in,
        send_sem=half_send, recv_sem=half_recv, device_id=(k, other, me), device_id_type=MESH)

    def work(slot, group):
        q = lax.div(group, PER_Q)
        at = lax.rem(group, PER_Q) * VEC
        wait_bytes(recv.at[slot, pl.ds(0, ORB - 1)], pair_recv.at[slot])
        for o in range(ORB):
            for e in range(PLANES - KEPT):
                for p in range(PIECES):
                    carrier = recv[slot, o, PIECES * e + p].astype(F32)
                    back = pltpu.roll(carrier, (128 - NORB + SPARE * p) % 128, 1)
                    value = jnp.where(lane >= SPARE * p, back, value) if p else back
                extra[o, e] = value.astype(BF16)

        def plane(j, ri):
            o, r = j // ROWS, j % ROWS
            f = ri * ROWS + r
            return recv[slot, o, f] if f < KEPT else extra[o, f - KEPT]

        for jb in range(PADDED // 16):
            rows = [j for j in range(16 * jb, 16 * jb + 16) if j < NORB]
            both = jnp.concatenate(
                [jnp.concatenate([plane(j, ri) for j in rows], axis=0) for ri in range(2)], axis=1)
            turned = jnp.dot(perm[:, 0:16 * len(rows)], both, preferred_element_type=F32).astype(BF16)
            for v in range(VEC):
                tile = turned[16 * v:16 * v + 16]
                flat[v, 16 * jb:16 * jb + 16, :] = tile
                rhs[16 * jb:16 * jb + 16, 256 * v:256 * v + 256] = tile
                rhs[128 + 16 * jb:144 + 16 * jb, 256 * v:256 * v + 128] = -tile[:, 128:256]
                rhs[128 + 16 * jb:144 + 16 * jb, 256 * v + 128:256 * v + 256] = tile[:, 0:128]

        step = 4
        for v in range(0, VEC, step):
            left = flat[v:v + step].reshape(step * PADDED, 256)
            for t in range(TAUS):
                y = jnp.dot(left, weights[q, :, 256 * t:256 * t + 256], preferred_element_type=F32)
                for i in range(step):
                    scale = screen_ref[q, t, at + v + i]
                    image[PADDED * t:PADDED * t + PADDED, 256 * (v + i):256 * (v + i) + 256] = (
                        y[PADDED * i:PADDED * i + PADDED] * scale).astype(BF16)

        def add(rows):
            total[rows] += lax.dot_general(
                image[rows], rhs[...], (((1,), (1,)), ((), ())), preferred_element_type=F32)

        @pl.when(slot != SLOTS - 1)
        def _():
            add(slice(None))

        @pl.when(slot == SLOTS - 1)
        def _():
            add(pl.ds(pl.multiple_of(other * half, half), half))
            swap_half.start()
            add(pl.ds(pl.multiple_of(core * half, half), half))

    def work_at(position, _):
        left_over = position == SLOTS // 2
        slot = jnp.where(left_over, SLOTS, jnp.where(position < SLOTS // 2, position, position - 1))
        number = ORB * SLOTS + jnp.where(me == first, 0, 1)
        group = jnp.where(left_over, number, me * SLOTS + slot)

        @pl.when(jnp.logical_not(left_over) | has_more)
        def _():
            work(slot, group)

        return 0

    lax.fori_loop(0, SLOTS + 1, work_at, 0)

    swap_half.wait()
    mine[...] = -(total[pl.ds(pl.multiple_of(core * half, half), half), :] + half_in[...])
    for d in (4, 5, 7, 6, 1, 3, 2, 0):
        to = peer(d)
        for t in range(2):
            base = pl.multiple_of(lax.div(ROWS * to, 8) * 8, 8)
            around = mine[pl.ds(t * PADDED + base, 24), :]
            rows = pltpu.roll(around, 24 - (ROWS * to - base), 0)[0:ROWS]
            for ri in range(2):
                at = ROWS * (2 * t + ri)
                piece[d, at:at + ROWS] = rows[:, 128 * ri:128 * ri + 128]
        if d:
            pltpu.make_async_remote_copy(
                src_ref=piece.at[d], dst_ref=gathered.at[me], send_sem=piece_send,
                recv_sem=piece_recv, device_id=(k, core, to), device_id_type=MESH).start()
    gathered[me] = piece[0]
    wait_bytes(gathered.at[pl.ds(0, ORB - 1)], piece_recv)
    summed = gathered[0]
    for o in range(1, ORB):
        summed = summed + gathered[o]
    result[...] = summed
    hand_over = pltpu.make_async_remote_copy(
        src_ref=result, dst_ref=result_in, send_sem=out_send, recv_sem=out_recv,
        device_id=(k, other, me), device_id_type=MESH)
    hand_over.start()

    def put_out(which, ref):
        for t in range(2):
            for ri in range(2):
                at = ROWS * (2 * t + ri)
                out_ref[2 * which + t, :, ri, :] = ref[at:at + ROWS, 0:NORB]

    put_out(core, result)

    wait_bytes(piece.at[pl.ds(0, ORB - 1)], piece_send)

    def sent_slot(slot, _):
        wait_bytes(recv.at[slot, pl.ds(0, ORB - 1)], pair_send.at[slot])
        return 0

    lax.fori_loop(0, SLOTS, sent_slot, 0)

    @pl.when(has_more)
    def _():
        wait_bytes(recv.at[SLOTS, pl.ds(0, 1)], pair_send.at[SLOTS])

    @pl.when(jnp.logical_not(has_more))
    def _():
        wait_bytes(recv.at[SLOTS, pl.ds(0, 2)], pair_send.at[SLOTS])

    @pl.when(core == 1)
    def _():
        wait_bytes(green_mine.at[pl.ds(0, ORB - 1)], gather_send)
        for q in range(2):
            wait_bytes(green_mine, shift_send.at[q])
        hand_green.wait_send()

    hand_over.wait()
    put_out(other, result_in)


def body(chol_pairs, green, screening):
    planes = jnp.transpose(chol_pairs[:, 0], (0, 1, 3, 2, 4))
    dma = pltpu.SemaphoreType.DMA
    out = pl.pallas_call(
        kernel,
        out_shape=jax.ShapeDtypeStruct((TAUS, ROWS, 2, NORB), F32),
        in_specs=[
            pl.BlockSpec(memory_space=pl.ANY),
            pl.BlockSpec(memory_space=pltpu.VMEM),
            pl.BlockSpec(memory_space=pltpu.SMEM),
        ],
        out_specs=pl.BlockSpec(memory_space=pltpu.VMEM),
        scratch_shapes=[
            pltpu.VMEM((2, 2, ROWS, PER_Q * VEC, NORB), BF16),
            pltpu.VMEM((ORB * SLOTS + 2, KEPT, VEC, 128), BF16),
            pltpu.VMEM((SLOTS + 1, ORB, KEPT, VEC, 128), BF16),
            pltpu.VMEM((ORB, PLANES - KEPT, VEC, 128), BF16),
            pltpu.VMEM((VEC, PADDED, 256), BF16),
            pltpu.VMEM((TAUS * PADDED, VEC * 256), BF16),
            pltpu.VMEM((256, VEC * 256), BF16),
            pltpu.VMEM((2, 256, TAUS * 256), BF16),
            pltpu.VMEM((256, 256), BF16),
            pltpu.VMEM((TAUS * PADDED, 256), F32),
            pltpu.VMEM((2 * PADDED, 256), F32),
            pltpu.VMEM((ORB, TAUS, ROWS, 2, NORB), BF16),
            pltpu.VMEM((2, ORB, TAUS, ROWS, 2, NORB), BF16),
            pltpu.VMEM((2 * PADDED, 256), F32),
            pltpu.VMEM((ORB, 56, 128), F32),
            pltpu.VMEM((ORB, 56, 128), F32),
            pltpu.VMEM((56, 128), F32),
            pltpu.VMEM((56, 128), F32),
            dma((2,)), pltpu.SemaphoreType.REGULAR, dma, dma, dma((2,)), dma((2,)), dma, dma,
            dma((SLOTS + 1,)), dma((SLOTS + 1,)),
            dma, dma, dma, dma, dma, dma,
        ],
        compiler_params=pltpu.CompilerParams(
            collective_id=0, has_side_effects=True, vmem_limit_bytes=56 * 1024 * 1024),
        cost_estimate=pl.CostEstimate(
            flops=7_200_000_000, bytes_accessed=5_400_000, transcendentals=0),
    )(planes, jnp.transpose(green[0], (0, 2, 1, 3)), screening)
    return jnp.transpose(out, (0, 2, 1, 3))[None]


def solution(mesh):
    placed = (
        P(None, "ka", None, "chol", "orb", None),
        P("ka", None, None, "orb", None),
        P(None, None, "chol"),
    )
    return jax.shard_map(
        body,
        mesh=mesh,
        in_specs=placed,
        out_specs=P("ka", None, None, "orb", None),
        check_vma=False,
    )
```

```python
import functools

import jax
import jax.numpy as jnp
from jax import lax
from jax.experimental import pallas as pl
from jax.experimental.pallas import tpu as pltpu
from jax.sharding import PartitionSpec as P

MESH = pl.DeviceIdType.MESH
BF16 = jnp.bfloat16
F32 = jnp.float32

ORB = 8
ROWS = 13
NORB = 104
PADDED = 112
TAUS = 4
VEC = 16
PER_Q = 25
SLOTS = 6
WHOLE = SLOTS - 1
HALF = VEC // 2
PLANES = 2 * ROWS
KEPT = 22
LAST = 20
SPARE = 128 - NORB
PIECES = 5


def pad_lanes(x):
    return jnp.concatenate([x, jnp.zeros((x.shape[0], 128 - x.shape[1]), x.dtype)], axis=1)


def kernel(
    chol_ref, green_ref, screen_ref, out_ref,
    loaded, send, send_last, send_over, recv, recv_last, recv_over, bank, extra, flat, image, rhs, weights, perm, total, mine,
    green_mine, green_all, half_in, piece, gathered, result, result_in,
    load_sem, ready, gather_send, gather_recv, shift_send, shift_recv, swap_send, swap_recv,
    pair_send, pair_recv, last_send, last_recv, over_send, over_recv, half_send, half_recv, piece_send, piece_recv, out_send, out_recv,
):
    k = lax.axis_index("ka")
    core = lax.axis_index("chol")
    me = lax.axis_index("orb")
    other = 1 - core
    has_over = lax.rem(me // 4 + lax.rem(me, 4), 2) == core
    over_at = me // 2
    half = 2 * PADDED

    def peer(d):
        dx, dy = d // 4, d % 4
        x = lax.rem(me // 4 + dx, 2)
        y = lax.rem(lax.rem(me, 4) + dy, 4)
        return x * 4 + y

    def load(q):
        return pltpu.make_async_copy(chol_ref.at[q], loaded.at[q], load_sem.at[q])

    def wait_bytes(ref, sem):
        pltpu.make_async_copy(ref, ref, sem).wait()

    for q in range(2):
        load(q).start()

    barrier = pltpu.get_barrier_semaphore()

    def greet(device):
        pl.semaphore_signal(barrier, inc=1, device_id=device, device_id_type=MESH)

    near_to = (lax.rem(k + 1, 8), core, peer(4))
    near_from = (lax.rem(k + 7, 8), core, peer(4))
    far = (lax.rem(k + 4, 8), core, me)
    for d in range(1, ORB):
        greet((k, 0, peer(d)))

    @pl.when(core == 1)
    def _():
        greet((k, 0, me))
        greet(near_to)
        greet(near_from)
        greet(far)

    lane = lax.broadcasted_iota(jnp.int32, (VEC, 128), 1)

    def plane_of(group):
        q = lax.div(group, PER_Q)
        at = pl.multiple_of(lax.rem(group, PER_Q) * VEC, VEC)

        def plane(f):
            return pad_lanes(loaded[q, f // ROWS, f % ROWS, pl.ds(at, VEC), :].astype(F32))

        return plane

    def fold(plane, kept, put):
        for e in range(4):
            riding = plane(kept + e)
            for p in range(PIECES):
                f = PIECES * e + p
                moved = pltpu.roll(riding, (NORB - SPARE * p) % 128, 1)
                put(f, jnp.where(lane < NORB, plane(f), moved))

    def fold_slot(slot, to, put):
        plane, plane_last = plane_of(to * SLOTS + slot), plane_of(to * SLOTS + WHOLE)
        fold(plane, KEPT, put)
        for e in range(2):
            moved = pltpu.roll(plane_last(LAST + 4 + e), NORB - SPARE * slot, 1)
            put(LAST + e, jnp.where(lane < NORB, plane(LAST + e), moved))

    def halves(put):
        held = {}

        def put_plane(f, value):
            held[f] = value
            if f ^ 1 in held:
                a, b = held[f & ~1], held[f | 1]
                for h in range(2):
                    rows = slice(HALF * h, HALF * h + HALF)
                    put(h, f // 2, jnp.concatenate([a[rows], b[rows]], axis=0).astype(BF16))

        return put_plane

    def send_slot(slot, _):
        def send_one(d, _):
            to = peer(d)

            def put(f, value):
                send[slot, d, f] = value.astype(BF16)

            fold_slot(slot, to, put)
            pltpu.make_async_remote_copy(
                src_ref=send.at[slot, d], dst_ref=recv.at[slot, me], send_sem=pair_send.at[slot],
                recv_sem=pair_recv.at[slot], device_id=(k, core, to), device_id_type=MESH).start()
            return 0

        lax.fori_loop(1, ORB, send_one, 0)

        def put_own(f, value):
            recv[slot, me, f] = value.astype(BF16)

        fold_slot(slot, me, put_own)
        return 0

    for q in range(2):
        load(q).wait()

    @pl.when(core == 0)
    def _():
        pl.semaphore_wait(barrier, 2 * ORB - 1)
        pl.semaphore_signal(ready, inc=1, device_id=(k, 1, me), device_id_type=MESH)

    @pl.when(core == 1)
    def _():
        pl.semaphore_wait(ready, 1)
        for d in range(1, ORB):
            pltpu.make_async_remote_copy(
                src_ref=green_ref, dst_ref=green_mine.at[me], send_sem=gather_send,
                recv_sem=gather_recv, device_id=(k, core, peer(d)), device_id_type=MESH).start()

    send_slot(0, 0)

    row = lax.broadcasted_iota(jnp.int32, (256, 256), 0)
    col = lax.broadcasted_iota(jnp.int32, (256, 256), 1)
    hit = (lax.div(row, 16) == lax.rem(col, 16)) & (lax.rem(row, 16) == lax.div(col, 16))
    perm[...] = jnp.where(hit, 1.0, 0.0).astype(BF16)
    for at in (PADDED, 128 + PADDED):
        rhs[at:at + 16, :] = jnp.zeros((16, VEC * 256), BF16)
    total[...] = jnp.zeros_like(total)
    weights[...] = jnp.zeros_like(weights)

    send_slot(1, 0)

    @pl.when(core == 1)
    def _():
        green_mine[me] = green_ref[...]
        wait_bytes(green_mine.at[pl.ds(0, ORB - 1)], gather_recv)
        pl.semaphore_wait(barrier, 3)
        for q, device in ((0, near_to), (1, far)):
            pltpu.make_async_remote_copy(
                src_ref=green_mine, dst_ref=green_all.at[q], send_sem=shift_send.at[q],
                recv_sem=shift_recv.at[q], device_id=device, device_id_type=MESH).start()

    lax.fori_loop(2, WHOLE, send_slot, 0)

    for number in range(2):
        plane = plane_of(ORB * SLOTS + number)

        def put_over(h, n, value, number=number):
            send_over[2 * number + h, n] = value

        put = halves(put_over)
        fold(plane, KEPT, put)
        for f in range(LAST, KEPT):
            put(f, plane(f))
    for number in range(4):
        to = 2 * number + lax.rem(core + number // 2, 2)

        @pl.when(me != to)
        def _(number=number, to=to):
            pltpu.make_async_remote_copy(
                src_ref=send_over.at[number], dst_ref=recv_over.at[me], send_sem=over_send,
                recv_sem=over_recv, device_id=(k, core, to), device_id_type=MESH).start()

        @pl.when(me == to)
        def _(number=number):
            recv_over[me] = send_over[number]

    def fold_last(d, _):
        def put_last(h, n, value):
            send_last[h, d, n] = value

        fold(plane_of(peer(d) * SLOTS + WHOLE), LAST, halves(put_last))
        return 0

    def send_last_half(h):
        def send_one(d, _):
            pltpu.make_async_remote_copy(
                src_ref=send_last.at[h, d], dst_ref=recv_last.at[h, me], send_sem=last_send.at[h],
                recv_sem=last_recv.at[h], device_id=(k, core, peer(d)), device_id_type=MESH).start()
            return 0

        lax.fori_loop(1, ORB, send_one, 0)

    lax.fori_loop(0, ORB, fold_last, 0)
    for h in range(2):
        send_last_half(h)
        recv_last[h, me] = send_last[h, 0]

    hand_green = pltpu.make_async_remote_copy(
        src_ref=green_all, dst_ref=green_all, send_sem=swap_send,
        recv_sem=swap_recv, device_id=(k, 0, me), device_id_type=MESH)

    @pl.when(core == 1)
    def _():
        for q in range(2):
            wait_bytes(green_all.at[q], shift_recv.at[q])
        hand_green.start()

    @pl.when(core == 0)
    def _():
        hand_green.wait_recv()

    for q in range(2):
        for t in range(TAUS):
            parts = []
            for ri in range(2):
                blocks = [green_all[q, o, t, :, ri, :].astype(F32) for o in range(ORB)]
                parts.append(pad_lanes(jnp.concatenate(blocks, axis=0)))
            at = t * 256
            real, imag = parts
            weights[q, 0:NORB, at:at + 128] = real.astype(BF16)
            weights[q, 0:NORB, at + 128:at + 256] = imag.astype(BF16)
            weights[q, 128:128 + NORB, at:at + 128] = (-imag).astype(BF16)
            weights[q, 128:128 + NORB, at + 128:at + 256] = real.astype(BF16)

    swap_half = pltpu.make_async_remote_copy(
        src_ref=total.at[pl.ds(pl.multiple_of(other * half, half), half)], dst_ref=half_in,
        send_sem=half_send, recv_sem=half_recv, device_id=(k, other, me), device_id_type=MESH)

    def unfold(planes, kept, o, put):
        for e in range(4):
            for p in range(PIECES):
                carrier = planes(PIECES * e + p).astype(F32)
                back = pltpu.roll(carrier, SPARE + SPARE * p, 1)
                value = jnp.where(lane >= SPARE * p, back, value) if p else back
            put(e, value.astype(BF16))

    def turn(plane, vectors):
        for jb in range(PADDED // 16):
            rows = [j for j in range(16 * jb, 16 * jb + 16) if j < NORB]
            both = jnp.concatenate(
                [jnp.concatenate([plane(j // ROWS, ri * ROWS + j % ROWS) for j in rows], axis=0)
                 for ri in range(2)], axis=1)
            turned = jnp.dot(perm[0:16 * vectors, 0:16 * len(rows)], both,
                             preferred_element_type=F32).astype(BF16)
            for v in range(vectors):
                tile = turned[16 * v:16 * v + 16]
                flat[v, 16 * jb:16 * jb + 16, :] = tile
                rhs[16 * jb:16 * jb + 16, 256 * v:256 * v + 256] = tile
                rhs[128 + 16 * jb:144 + 16 * jb, 256 * v:256 * v + 128] = -tile[:, 128:256]
                rhs[128 + 16 * jb:144 + 16 * jb, 256 * v + 128:256 * v + 256] = tile[:, 0:128]

    def image_of(q, at, vectors):
        step = 4
        for v in range(0, vectors, step):
            left = flat[v:v + step].reshape(step * PADDED, 256)
            for t in range(TAUS):
                y = jnp.dot(left, weights[q, :, 256 * t:256 * t + 256], preferred_element_type=F32)
                for i in range(step):
                    scale = screen_ref[q, t, at + v + i]
                    image[PADDED * t:PADDED * t + PADDED, 256 * (v + i):256 * (v + i) + 256] = (
                        y[PADDED * i:PADDED * i + PADDED] * scale).astype(BF16)

    def add(rows, vectors):
        cols = slice(0, 256 * vectors)
        total[rows] += lax.dot_general(
            image[rows, cols], rhs[:, cols], (((1,), (1,)), ((), ())), preferred_element_type=F32)

    def work_whole(slot, _):
        group = me * SLOTS + slot
        wait_bytes(recv.at[slot, pl.ds(0, ORB - 1)], pair_recv.at[slot])
        for o in range(ORB):
            def put(e, value, o=o):
                extra[o, e] = value

            unfold(lambda f, o=o: recv[slot, o, f], KEPT, o, put)
        turn(lambda o, f: recv[slot, o, f] if f < KEPT else extra[o, f - KEPT], VEC)
        image_of(lax.div(group, PER_Q), lax.rem(group, PER_Q) * VEC, VEC)
        add(slice(None), VEC)
        return 0

    def turned_over(value):
        return jnp.concatenate([value[HALF:], value[:HALF]], axis=0)

    def unpack(tiles, kept):
        for o in range(ORB):
            for n in range(kept // 2):
                tile = tiles(o, n)
                bank[o, 2 * n] = tile
                bank[o, 2 * n + 1] = turned_over(tile.astype(F32)).astype(BF16)

            def put(e, value, o=o):
                bank[o, kept + e] = value

            unfold(lambda f, o=o: bank[o, f], kept, o, put)

    def work_half(position, _):
        h = jnp.where(position == 0, lax.rem(over_at, 2), position - 1)
        group = jnp.where(position == 0, ORB * SLOTS + over_at // 2, me * SLOTS + WHOLE)

        @pl.when(position == 0)
        def _():
            wait_bytes(recv_over.at[pl.ds(0, ORB - 1)], over_recv)
            unpack(lambda o, n: recv_over[o, n], KEPT)

        @pl.when(position != 0)
        def _():
            wait_bytes(recv_last.at[h, pl.ds(0, ORB - 1)], last_recv.at[h])
            unpack(lambda o, n: recv_last[h, o, n], LAST)
            for o in range(ORB):
                for e in range(2):
                    for p in range(PIECES):
                        back = pltpu.roll(recv[p, o, LAST + e].astype(F32), SPARE + SPARE * p, 1)
                        value = jnp.where(lane >= SPARE * p, back, value) if p else back
                    bank[o, LAST + 4 + e] = jnp.where(h == 1, turned_over(value), value).astype(BF16)

        turn(lambda o, f: bank[o, f], HALF)
        image_of(lax.div(group, PER_Q), lax.rem(group, PER_Q) * VEC + HALF * h, HALF)

        @pl.when(position != 2)
        def _():
            add(slice(None), HALF)

        @pl.when(position == 2)
        def _():
            add(pl.ds(pl.multiple_of(other * half, half), half), HALF)
            swap_half.start()
            add(pl.ds(pl.multiple_of(core * half, half), half), HALF)

        return 0

    lax.fori_loop(0, WHOLE, work_whole, 0)
    lax.fori_loop(jnp.where(has_over, 0, 1), 3, work_half, 0)

    swap_half.wait()
    mine[...] = -(total[pl.ds(pl.multiple_of(core * half, half), half), :] + half_in[...])
    for d in (4, 5, 7, 6, 1, 3, 2, 0):
        to = peer(d)
        for t in range(2):
            base = pl.multiple_of(lax.div(ROWS * to, 8) * 8, 8)
            around = mine[pl.ds(t * PADDED + base, 24), :]
            rows = pltpu.roll(around, 24 - (ROWS * to - base), 0)[0:ROWS]
            for ri in range(2):
                at = ROWS * (2 * t + ri)
                piece[d, at:at + ROWS] = rows[:, 128 * ri:128 * ri + 128]
        if d:
            pltpu.make_async_remote_copy(
                src_ref=piece.at[d], dst_ref=gathered.at[me], send_sem=piece_send,
                recv_sem=piece_recv, device_id=(k, core, to), device_id_type=MESH).start()
    gathered[me] = piece[0]
    wait_bytes(gathered.at[pl.ds(0, ORB - 1)], piece_recv)
    summed = gathered[0]
    for o in range(1, ORB):
        summed = summed + gathered[o]
    result[...] = summed
    hand_over = pltpu.make_async_remote_copy(
        src_ref=result, dst_ref=result_in, send_sem=out_send, recv_sem=out_recv,
        device_id=(k, other, me), device_id_type=MESH)
    hand_over.start()

    def put_out(which, ref):
        for t in range(2):
            for ri in range(2):
                at = ROWS * (2 * t + ri)
                out_ref[2 * which + t, :, ri, :] = ref[at:at + ROWS, 0:NORB]

    put_out(core, result)

    wait_bytes(piece.at[pl.ds(0, ORB - 1)], piece_send)

    def sent_slot(slot, _):
        wait_bytes(recv.at[slot, pl.ds(0, ORB - 1)], pair_send.at[slot])
        return 0

    lax.fori_loop(0, WHOLE, sent_slot, 0)
    for h in range(2):
        wait_bytes(recv_last.at[h, pl.ds(0, ORB - 1)], last_send.at[h])

    @pl.when(has_over)
    def _():
        wait_bytes(recv_over.at[pl.ds(0, 3)], over_send)

    @pl.when(jnp.logical_not(has_over))
    def _():
        wait_bytes(recv_over.at[pl.ds(0, 4)], over_send)

    @pl.when(core == 1)
    def _():
        wait_bytes(green_mine.at[pl.ds(0, ORB - 1)], gather_send)
        for q in range(2):
            wait_bytes(green_mine, shift_send.at[q])
        hand_green.wait_send()

    hand_over.wait()
    put_out(other, result_in)


def body(chol_pairs, green, screening):
    planes = jnp.transpose(chol_pairs[:, 0], (0, 1, 3, 2, 4))
    dma = pltpu.SemaphoreType.DMA
    out = pl.pallas_call(
        kernel,
        out_shape=pltpu.VMEM((TAUS, ROWS, 2, NORB), F32),
        in_specs=[
            pl.BlockSpec(memory_space=pl.ANY),
            pl.BlockSpec(memory_space=pltpu.VMEM),
            pl.BlockSpec(memory_space=pltpu.SMEM),
        ],
        out_specs=pl.BlockSpec(memory_space=pltpu.VMEM),
        scratch_shapes=[
            pltpu.VMEM((2, 2, ROWS, PER_Q * VEC, NORB), BF16),
            pltpu.VMEM((WHOLE, ORB, KEPT, VEC, 128), BF16),
            pltpu.VMEM((2, ORB, LAST // 2, VEC, 128), BF16),
            pltpu.VMEM((4, KEPT // 2, VEC, 128), BF16),
            pltpu.VMEM((WHOLE, ORB, KEPT, VEC, 128), BF16),
            pltpu.VMEM((2, ORB, LAST // 2, VEC, 128), BF16),
            pltpu.VMEM((ORB, KEPT // 2, VEC, 128), BF16),
            pltpu.VMEM((ORB, PLANES, VEC, 128), BF16),
            pltpu.VMEM((ORB, PLANES - KEPT, VEC, 128), BF16),
            pltpu.VMEM((VEC, PADDED, 256), BF16),
            pltpu.VMEM((TAUS * PADDED, VEC * 256), BF16),
            pltpu.VMEM((256, VEC * 256), BF16),
            pltpu.VMEM((2, 256, TAUS * 256), BF16),
            pltpu.VMEM((256, 256), BF16),
            pltpu.VMEM((TAUS * PADDED, 256), F32),
            pltpu.VMEM((2 * PADDED, 256), F32),
            pltpu.VMEM((ORB, TAUS, ROWS, 2, NORB), BF16),
            pltpu.VMEM((2, ORB, TAUS, ROWS, 2, NORB), BF16),
            pltpu.VMEM((2 * PADDED, 256), F32),
            pltpu.VMEM((ORB, 56, 128), F32),
            pltpu.VMEM((ORB, 56, 128), F32),
            pltpu.VMEM((56, 128), F32),
            pltpu.VMEM((56, 128), F32),
            dma((2,)), pltpu.SemaphoreType.REGULAR, dma, dma, dma((2,)), dma((2,)), dma, dma,
            dma((WHOLE,)), dma((WHOLE,)), dma((2,)), dma((2,)), dma, dma,
            dma, dma, dma, dma, dma, dma,
        ],
        compiler_params=pltpu.CompilerParams(
            collective_id=0, has_side_effects=True, vmem_limit_bytes=56 * 1024 * 1024),
        cost_estimate=pl.CostEstimate(
            flops=7_200_000_000, bytes_accessed=5_400_000, transcendentals=0),
    )(planes, jnp.transpose(green[0], (0, 2, 1, 3)), screening)
    return jnp.transpose(out, (0, 2, 1, 3))[None]


def solution(mesh):
    placed = (
        P(None, "ka", None, "chol", "orb", None),
        P("ka", None, None, "orb", None),
        P(None, None, "chol"),
    )
    return jax.shard_map(
        body,
        mesh=mesh,
        in_specs=placed,
        out_specs=P("ka", None, None, "orb", None),
        check_vma=False,
    )
```

```python
import functools

import jax
import jax.numpy as jnp
from jax import lax
from jax.experimental import pallas as pl
from jax.experimental.pallas import tpu as pltpu
from jax.sharding import PartitionSpec as P

MESH = pl.DeviceIdType.MESH
BF16 = jnp.bfloat16
F32 = jnp.float32

ORB = 8
ROWS = 13
NORB = 104
PADDED = 112
TAUS = 4
VEC = 16
PER_Q = 25
SLOTS = 6
WHOLE = SLOTS - 1
HALF = VEC // 2
PLANES = 2 * ROWS
KEPT = 22
LAST = 18
ALONG = LAST + 4
THIN = 16
SPARE = 128 - NORB
PIECES = 5


def pad_lanes(x):
    return jnp.concatenate([x, jnp.zeros((x.shape[0], 128 - x.shape[1]), x.dtype)], axis=1)


def kernel(
    chol_ref, green_ref, screen_ref, out_ref,
    loaded, first, first_along, send, send_last, send_over, recv, recv_last, recv_over, bank, extra, flat, image, rhs, weights, perm, total, mine,
    green_mine, green_all, half_in, piece, gathered, result, result_in,
    load_sem, first_sem, ready, gather_send, gather_recv, shift_send, shift_recv, swap_send, swap_recv,
    pair_send, pair_recv, last_send, last_recv, over_send, over_recv, half_send, half_recv, piece_send, piece_recv, out_send, out_recv,
):
    k = lax.axis_index("ka")
    core = lax.axis_index("chol")
    me = lax.axis_index("orb")
    other = 1 - core
    has_over = lax.rem(me // 4 + lax.rem(me, 4), 2) == core
    over_at = me // 2
    half = 2 * PADDED

    def peer(d):
        dx, dy = d // 4, d % 4
        x = lax.rem(me // 4 + dx, 2)
        y = lax.rem(lax.rem(me, 4) + dy, 4)
        return x * 4 + y

    def place(group):
        q = lax.div(group, PER_Q)
        return q, pl.multiple_of(lax.rem(group, PER_Q) * VEC, VEC)

    def load(q):
        return pltpu.make_async_copy(chol_ref.at[q], loaded.at[q], load_sem.at[q])

    def wait_bytes(ref, sem):
        pltpu.make_async_copy(ref, ref, sem).wait()

    barrier = pltpu.get_barrier_semaphore()

    def greet(device):
        pl.semaphore_signal(barrier, inc=1, device_id=device, device_id_type=MESH)

    near_to = (lax.rem(k + 1, 8), core, peer(4))
    near_from = (lax.rem(k + 7, 8), core, peer(4))
    far = (lax.rem(k + 4, 8), core, me)
    for d in range(1, ORB):
        greet((k, 0, peer(d)))

    @pl.when(core == 1)
    def _():
        greet((k, 0, me))
        greet(near_to)
        greet(near_from)
        greet(far)

    for d in range(ORB):
        q, at = place(peer(d) * SLOTS)
        pltpu.make_async_copy(
            chol_ref.at[q, :, :, pl.ds(at, VEC), :], first.at[d], first_sem.at[0]).start()
        q, at = place(peer(d) * SLOTS + WHOLE)
        pltpu.make_async_copy(
            chol_ref.at[q, 1, pl.ds(ALONG - ROWS, 4), pl.ds(at, VEC), :], first_along.at[d],
            first_sem.at[1]).start()

    lane = lax.broadcasted_iota(jnp.int32, (VEC, 128), 1)

    def plane_of(group):
        q, at = place(group)

        def plane(f):
            return pad_lanes(loaded[q, f // ROWS, f % ROWS, pl.ds(at, VEC), :].astype(F32))

        return plane

    def along_of(group):
        q, at = place(group)

        def plane(n):
            return pad_lanes(loaded[q, 1, ALONG - ROWS + n, pl.ds(at, VEC), :].astype(F32))

        return plane

    def fold(plane, put, thin=None):
        for e in range(4):
            riding = plane(KEPT + e)
            for p in range(PIECES):
                f = PIECES * e + p
                moved = pltpu.roll(riding, (NORB - SPARE * p) % 128, 1)
                value = jnp.where(lane < NORB, plane(f), moved)
                if p == PIECES - 1 and thin is not None:
                    value = jnp.where(lane < 128 - THIN, value, thin(e))
                put(f, value)

    def fold_slot(slot, plane, along, put):
        def thin(e):
            number = 4 * slot + e
            which = jnp.where(number < 7, 0, 1)
            piece_at = lax.rem(number, 7)
            return pltpu.roll(along(which), lax.rem(128 + 128 - THIN - THIN * piece_at, 128), 1)

        fold(plane, put, thin)
        for e in range(2):
            f = PIECES * 4 + e
            moved = pltpu.roll(along(2 + e), NORB - SPARE * slot, 1)
            put(f, jnp.where(lane < NORB, plane(f), moved))

    def fold_tail(plane, put):
        riders = [plane(LAST + e) for e in range(4)]
        for e in range(4):
            for p in range(4):
                moved = pltpu.roll(riders[e], (NORB - SPARE * p) % 128, 1)
                put(4 * e + p, jnp.where(lane < NORB, plane(4 * e + p), moved))
        value = plane(16)
        for e in range(3):
            value = jnp.where(lane < NORB + 8 * e, value, pltpu.roll(riders[e], 8 + 8 * e, 1))
        put(16, value)
        put(17, jnp.where(lane < NORB, plane(17), pltpu.roll(riders[3], 8, 1)))

    def halves(put):
        held = {}

        def put_plane(f, value):
            held[f] = value
            if f ^ 1 in held:
                a, b = held[f & ~1], held[f | 1]
                for h in range(2):
                    rows = slice(HALF * h, HALF * h + HALF)
                    put(h, f // 2, jnp.concatenate([a[rows], b[rows]], axis=0).astype(BF16))

        return put_plane

    def send_slot(slot, _, early=False):
        def sources(d):
            if early:
                return (lambda f: pad_lanes(first[d, f // ROWS, f % ROWS].astype(F32)),
                        lambda n: pad_lanes(first_along[d, n].astype(F32)))
            group = peer(d) * SLOTS
            return plane_of(group + slot), along_of(group + WHOLE)

        def send_one(n, _):
            d = ORB - n
            to = peer(d)

            def put(f, value):
                send[slot, d, f] = value.astype(BF16)

            fold_slot(slot, *sources(d), put)
            pltpu.make_async_remote_copy(
                src_ref=send.at[slot, d], dst_ref=recv.at[slot, me], send_sem=pair_send.at[slot],
                recv_sem=pair_recv.at[slot], device_id=(k, core, to), device_id_type=MESH).start()
            return 0

        lax.fori_loop(1, ORB, send_one, 0)

        def put_own(f, value):
            recv[slot, me, f] = value.astype(BF16)

        fold_slot(slot, *sources(0), put_own)
        return 0

    wait_bytes(first, first_sem.at[0])
    wait_bytes(first_along, first_sem.at[1])
    for q in range(2):
        load(q).start()

    @pl.when(core == 0)
    def _():
        pl.semaphore_wait(barrier, 2 * ORB - 1)
        pl.semaphore_signal(ready, inc=1, device_id=(k, 1, me), device_id_type=MESH)

    @pl.when(core == 1)
    def _():
        pl.semaphore_wait(ready, 1)
        for d in range(1, ORB):
            pltpu.make_async_remote_copy(
                src_ref=green_ref, dst_ref=green_mine.at[me], send_sem=gather_send,
                recv_sem=gather_recv, device_id=(k, core, peer(d)), device_id_type=MESH).start()

    send_slot(0, 0, early=True)

    row = lax.broadcasted_iota(jnp.int32, (256, 256), 0)
    col = lax.broadcasted_iota(jnp.int32, (256, 256), 1)
    hit = (lax.div(row, 16) == lax.rem(col, 16)) & (lax.rem(row, 16) == lax.div(col, 16))
    perm[...] = jnp.where(hit, 1.0, 0.0).astype(BF16)
    for at in (PADDED, 128 + PADDED):
        rhs[at:at + 16, :] = jnp.zeros((16, VEC * 256), BF16)
    total[...] = jnp.zeros_like(total)
    weights[...] = jnp.zeros_like(weights)

    for q in range(2):
        load(q).wait()
    send_slot(1, 0)

    @pl.when(core == 1)
    def _():
        green_mine[me] = green_ref[...]
        wait_bytes(green_mine.at[pl.ds(0, ORB - 1)], gather_recv)
        pl.semaphore_wait(barrier, 3)
        for q, device in ((0, near_to), (1, far)):
            pltpu.make_async_remote_copy(
                src_ref=green_mine, dst_ref=green_all.at[q], send_sem=shift_send.at[q],
                recv_sem=shift_recv.at[q], device_id=device, device_id_type=MESH).start()

    lax.fori_loop(2, WHOLE, send_slot, 0)

    for number in range(2):
        plane = plane_of(ORB * SLOTS + number)

        def put_over(h, n, value, number=number):
            send_over[2 * number + h, n] = value

        put = halves(put_over)
        fold(plane, put)
        for f in range(PIECES * 4, KEPT):
            put(f, plane(f))
    for number in range(4):
        to = 2 * number + lax.rem(core + number // 2, 2)

        @pl.when(me != to)
        def _(number=number, to=to):
            pltpu.make_async_remote_copy(
                src_ref=send_over.at[number], dst_ref=recv_over.at[me], send_sem=over_send,
                recv_sem=over_recv, device_id=(k, core, to), device_id_type=MESH).start()

        @pl.when(me == to)
        def _(number=number):
            recv_over[me] = send_over[number]

    def fold_last(d, _):
        def put_last(h, n, value):
            send_last[h, d, n] = value

        fold_tail(plane_of(peer(d) * SLOTS + WHOLE), halves(put_last))
        return 0

    def send_last_half(h):
        def send_one(n, _):
            d = ORB - n
            pltpu.make_async_remote_copy(
                src_ref=send_last.at[h, d], dst_ref=recv_last.at[h, me], send_sem=last_send.at[h],
                recv_sem=last_recv.at[h], device_id=(k, core, peer(d)), device_id_type=MESH).start()
            return 0

        lax.fori_loop(1, ORB, send_one, 0)

    lax.fori_loop(0, ORB, fold_last, 0)
    for h in range(2):
        send_last_half(h)
        recv_last[h, me] = send_last[h, 0]

    hand_green = pltpu.make_async_remote_copy(
        src_ref=green_all, dst_ref=green_all, send_sem=swap_send,
        recv_sem=swap_recv, device_id=(k, 0, me), device_id_type=MESH)

    @pl.when(core == 1)
    def _():
        for q in range(2):
            wait_bytes(green_all.at[q], shift_recv.at[q])
        hand_green.start()

    @pl.when(core == 0)
    def _():
        hand_green.wait_recv()

    for q in range(2):
        for t in range(TAUS):
            parts = []
            for ri in range(2):
                blocks = [green_all[q, o, t, :, ri, :].astype(F32) for o in range(ORB)]
                parts.append(pad_lanes(jnp.concatenate(blocks, axis=0)))
            at = t * 256
            real, imag = parts
            weights[q, 0:NORB, at:at + 128] = real.astype(BF16)
            weights[q, 0:NORB, at + 128:at + 256] = imag.astype(BF16)
            weights[q, 128:128 + NORB, at:at + 128] = (-imag).astype(BF16)
            weights[q, 128:128 + NORB, at + 128:at + 256] = real.astype(BF16)

    swap_half = pltpu.make_async_remote_copy(
        src_ref=total.at[pl.ds(pl.multiple_of(other * half, half), half)], dst_ref=half_in,
        send_sem=half_send, recv_sem=half_recv, device_id=(k, other, me), device_id_type=MESH)

    def pieced(pieces):
        for n, (tile, by, start) in enumerate(pieces):
            back = pltpu.roll(tile.astype(F32), by, 1)
            value = jnp.where(lane >= start, back, value) if n else back
        return value

    def unfold(planes, put):
        for e in range(4):
            put(e, pieced([
                (planes(PIECES * e + p), SPARE + SPARE * p, SPARE * p) for p in range(PIECES)
            ]).astype(BF16))

    def unfold_tail(planes, put):
        for e in range(4):
            pieces = [(planes(4 * e + p), SPARE + SPARE * p, SPARE * p) for p in range(4)]
            pieces.append((planes(16), 120 - 8 * e, 96) if e < 3 else (planes(17), 120, 96))
            put(e, pieced(pieces).astype(BF16))

    def turn(plane, vectors):
        for jb in range(PADDED // 16):
            rows = [j for j in range(16 * jb, 16 * jb + 16) if j < NORB]
            both = jnp.concatenate(
                [jnp.concatenate([plane(j // ROWS, ri * ROWS + j % ROWS) for j in rows], axis=0)
                 for ri in range(2)], axis=1)
            turned = jnp.dot(perm[0:16 * vectors, 0:16 * len(rows)], both,
                             preferred_element_type=F32).astype(BF16)
            for v in range(vectors):
                tile = turned[16 * v:16 * v + 16]
                flat[v, 16 * jb:16 * jb + 16, :] = tile
                rhs[16 * jb:16 * jb + 16, 256 * v:256 * v + 256] = tile
                rhs[128 + 16 * jb:144 + 16 * jb, 256 * v:256 * v + 128] = -tile[:, 128:256]
                rhs[128 + 16 * jb:144 + 16 * jb, 256 * v + 128:256 * v + 256] = tile[:, 0:128]

    def image_of(q, at, vectors):
        step = 4
        for v in range(0, vectors, step):
            left = flat[v:v + step].reshape(step * PADDED, 256)
            for t in range(TAUS):
                y = jnp.dot(left, weights[q, :, 256 * t:256 * t + 256], preferred_element_type=F32)
                for i in range(step):
                    scale = screen_ref[q, t, at + v + i]
                    image[PADDED * t:PADDED * t + PADDED, 256 * (v + i):256 * (v + i) + 256] = (
                        y[PADDED * i:PADDED * i + PADDED] * scale).astype(BF16)

    def add(rows, vectors):
        cols = slice(0, 256 * vectors)
        total[rows] += lax.dot_general(
            image[rows, cols], rhs[:, cols], (((1,), (1,)), ((), ())), preferred_element_type=F32)

    def work_whole(slot, _):
        group = me * SLOTS + slot
        wait_bytes(recv.at[slot, pl.ds(0, ORB - 1)], pair_recv.at[slot])
        for o in range(ORB):
            def put(e, value, o=o):
                extra[o, e] = value

            unfold(lambda f, o=o: recv[slot, o, f], put)
        turn(lambda o, f: recv[slot, o, f] if f < KEPT else extra[o, f - KEPT], VEC)
        image_of(lax.div(group, PER_Q), lax.rem(group, PER_Q) * VEC, VEC)
        add(slice(None), VEC)
        return 0

    def turned_over(value):
        return jnp.concatenate([value[HALF:], value[:HALF]], axis=0)

    def unpack(tiles, kept, spread):
        for o in range(ORB):
            for n in range(kept // 2):
                tile = tiles(o, n)
                bank[o, 2 * n] = tile
                bank[o, 2 * n + 1] = turned_over(tile.astype(F32)).astype(BF16)

            def put(e, value, o=o):
                bank[o, kept + e] = value

            spread(lambda f, o=o: bank[o, f], put)

    def along_planes(o):
        for a in range(2):
            pieces = [divmod(7 * a + m, 4) for m in range(7)]
            yield pieced([(recv[p, o, PIECES * e + 4], THIN + THIN * m, THIN * m)
                          for m, (p, e) in enumerate(pieces)])
        for e in range(2):
            yield pieced([(recv[p, o, 20 + e], SPARE + SPARE * p, SPARE * p) for p in range(WHOLE)])

    def work_half(position, _):
        h = jnp.where(position == 0, lax.rem(over_at, 2), position - 1)
        group = jnp.where(position == 0, ORB * SLOTS + over_at // 2, me * SLOTS + WHOLE)

        @pl.when(position == 0)
        def _():
            wait_bytes(recv_over.at[pl.ds(0, ORB - 1)], over_recv)
            unpack(lambda o, n: recv_over[o, n], KEPT, unfold)

        @pl.when(position != 0)
        def _():
            for o in range(ORB):
                for n, value in enumerate(along_planes(o)):
                    bank[o, ALONG + n] = jnp.where(h == 1, turned_over(value), value).astype(BF16)
            wait_bytes(recv_last.at[h, pl.ds(0, ORB - 1)], last_recv.at[h])
            unpack(lambda o, n: recv_last[h, o, n], LAST, unfold_tail)

        turn(lambda o, f: bank[o, f], HALF)
        image_of(lax.div(group, PER_Q), lax.rem(group, PER_Q) * VEC + HALF * h, HALF)

        @pl.when(position != 2)
        def _():
            add(slice(None), HALF)

        @pl.when(position == 2)
        def _():
            add(pl.ds(pl.multiple_of(other * half, half), half), HALF)
            swap_half.start()
            add(pl.ds(pl.multiple_of(core * half, half), half), HALF)

        return 0

    lax.fori_loop(0, WHOLE, work_whole, 0)
    lax.fori_loop(jnp.where(has_over, 0, 1), 3, work_half, 0)

    swap_half.wait()
    mine[...] = -(total[pl.ds(pl.multiple_of(core * half, half), half), :] + half_in[...])
    for d in (4, 5, 7, 6, 1, 3, 2, 0):
        to = peer(d)
        for t in range(2):
            base = pl.multiple_of(lax.div(ROWS * to, 8) * 8, 8)
            around = mine[pl.ds(t * PADDED + base, 24), :]
            rows = pltpu.roll(around, 24 - (ROWS * to - base), 0)[0:ROWS]
            for ri in range(2):
                at = ROWS * (2 * t + ri)
                piece[d, at:at + ROWS] = rows[:, 128 * ri:128 * ri + 128]
        if d:
            pltpu.make_async_remote_copy(
                src_ref=piece.at[d], dst_ref=gathered.at[me], send_sem=piece_send,
                recv_sem=piece_recv, device_id=(k, core, to), device_id_type=MESH).start()
    gathered[me] = piece[0]
    wait_bytes(gathered.at[pl.ds(0, ORB - 1)], piece_recv)
    summed = gathered[0]
    for o in range(1, ORB):
        summed = summed + gathered[o]
    result[...] = summed
    hand_over = pltpu.make_async_remote_copy(
        src_ref=result, dst_ref=result_in, send_sem=out_send, recv_sem=out_recv,
        device_id=(k, other, me), device_id_type=MESH)
    hand_over.start()

    def put_out(which, ref):
        for t in range(2):
            for ri in range(2):
                at = ROWS * (2 * t + ri)
                out_ref[2 * which + t, :, ri, :] = ref[at:at + ROWS, 0:NORB]

    put_out(core, result)

    wait_bytes(piece.at[pl.ds(0, ORB - 1)], piece_send)

    def sent_slot(slot, _):
        wait_bytes(recv.at[slot, pl.ds(0, ORB - 1)], pair_send.at[slot])
        return 0

    lax.fori_loop(0, WHOLE, sent_slot, 0)
    for h in range(2):
        wait_bytes(recv_last.at[h, pl.ds(0, ORB - 1)], last_send.at[h])

    @pl.when(has_over)
    def _():
        wait_bytes(recv_over.at[pl.ds(0, 3)], over_send)

    @pl.when(jnp.logical_not(has_over))
    def _():
        wait_bytes(recv_over.at[pl.ds(0, 4)], over_send)

    @pl.when(core == 1)
    def _():
        wait_bytes(green_mine.at[pl.ds(0, ORB - 1)], gather_send)
        for q in range(2):
            wait_bytes(green_mine, shift_send.at[q])
        hand_green.wait_send()

    hand_over.wait()
    put_out(other, result_in)


def body(chol_pairs, green, screening):
    planes = jnp.transpose(chol_pairs[:, 0], (0, 1, 3, 2, 4))
    dma = pltpu.SemaphoreType.DMA
    out = pl.pallas_call(
        kernel,
        out_shape=pltpu.VMEM((TAUS, ROWS, 2, NORB), F32),
        in_specs=[
            pl.BlockSpec(memory_space=pl.ANY),
            pl.BlockSpec(memory_space=pltpu.VMEM),
            pl.BlockSpec(memory_space=pltpu.SMEM),
        ],
        out_specs=pl.BlockSpec(memory_space=pltpu.VMEM),
        scratch_shapes=[
            pltpu.VMEM((2, 2, ROWS, PER_Q * VEC, NORB), BF16),
            pltpu.VMEM((ORB, 2, ROWS, VEC, NORB), BF16),
            pltpu.VMEM((ORB, 4, VEC, NORB), BF16),
            pltpu.VMEM((WHOLE, ORB, KEPT, VEC, 128), BF16),
            pltpu.VMEM((2, ORB, LAST // 2, VEC, 128), BF16),
            pltpu.VMEM((4, KEPT // 2, VEC, 128), BF16),
            pltpu.VMEM((WHOLE, ORB, KEPT, VEC, 128), BF16),
            pltpu.VMEM((2, ORB, LAST // 2, VEC, 128), BF16),
            pltpu.VMEM((ORB, KEPT // 2, VEC, 128), BF16),
            pltpu.VMEM((ORB, PLANES, VEC, 128), BF16),
            pltpu.VMEM((ORB, PLANES - KEPT, VEC, 128), BF16),
            pltpu.VMEM((VEC, PADDED, 256), BF16),
            pltpu.VMEM((TAUS * PADDED, VEC * 256), BF16),
            pltpu.VMEM((256, VEC * 256), BF16),
            pltpu.VMEM((2, 256, TAUS * 256), BF16),
            pltpu.VMEM((256, 256), BF16),
            pltpu.VMEM((TAUS * PADDED, 256), F32),
            pltpu.VMEM((2 * PADDED, 256), F32),
            pltpu.VMEM((ORB, TAUS, ROWS, 2, NORB), BF16),
            pltpu.VMEM((2, ORB, TAUS, ROWS, 2, NORB), BF16),
            pltpu.VMEM((2 * PADDED, 256), F32),
            pltpu.VMEM((ORB, 56, 128), F32),
            pltpu.VMEM((ORB, 56, 128), F32),
            pltpu.VMEM((56, 128), F32),
            pltpu.VMEM((56, 128), F32),
            dma((2,)), dma((2,)), pltpu.SemaphoreType.REGULAR, dma, dma, dma((2,)), dma((2,)), dma, dma,
            dma((WHOLE,)), dma((WHOLE,)), dma((2,)), dma((2,)), dma, dma,
            dma, dma, dma, dma, dma, dma,
        ],
        compiler_params=pltpu.CompilerParams(
            collective_id=0, has_side_effects=True, vmem_limit_bytes=56 * 1024 * 1024),
        cost_estimate=pl.CostEstimate(
            flops=7_200_000_000, bytes_accessed=5_400_000, transcendentals=0),
    )(planes, jnp.transpose(green[0], (0, 2, 1, 3)), screening)
    return jnp.transpose(out, (0, 2, 1, 3))[None]


def solution(mesh):
    placed = (
        P(None, "ka", None, "chol", "orb", None),
        P("ka", None, None, "orb", None),
        P(None, None, "chol"),
    )
    return jax.shard_map(
        body,
        mesh=mesh,
        in_specs=placed,
        out_specs=P("ka", None, None, "orb", None),
        check_vma=False,
    )
```

```python
import functools

import jax
import jax.numpy as jnp
from jax import lax
from jax.experimental import pallas as pl
from jax.experimental.pallas import tpu as pltpu
from jax.sharding import PartitionSpec as P

MESH = pl.DeviceIdType.MESH
BF16 = jnp.bfloat16
F32 = jnp.float32

ORB = 8
ROWS = 13
NORB = 104
PADDED = 112
TAUS = 4
VEC = 16
PER_Q = 25
SLOTS = 6
WHOLE = SLOTS - 1
HALF = VEC // 2
PLANES = 2 * ROWS
KEPT = 22
LAST = 18
ALONG = LAST + 4
THIN = 16
SPARE = 128 - NORB
PIECES = 5


def pad_lanes(x):
    return jnp.concatenate([x, jnp.zeros((x.shape[0], 128 - x.shape[1]), x.dtype)], axis=1)


def kernel(
    chol_ref, green_ref, screen_ref, out_ref,
    loaded, first, first_along, send, send_last, send_over, recv, recv_last, recv_over, bank, extra, flat, image, rhs, weights, perm, total, mine,
    green_mine, green_all, half_in, cut, piece, gathered, result, result_in,
    load_sem, first_sem, ready, gather_send, gather_recv, shift_send, shift_recv, swap_send, swap_recv,
    pair_send, pair_recv, last_send, last_recv, over_send, over_recv, half_send, half_recv, piece_send, piece_recv, out_send, out_recv,
):
    k = lax.axis_index("ka")
    core = lax.axis_index("chol")
    me = lax.axis_index("orb")
    other = 1 - core
    has_over = lax.rem(me // 4 + lax.rem(me, 4), 2) == core
    over_at = me // 2
    half = 2 * PADDED

    def peer(d):
        dx, dy = d // 4, d % 4
        x = lax.rem(me // 4 + dx, 2)
        y = lax.rem(lax.rem(me, 4) + dy, 4)
        return x * 4 + y

    def place(group):
        q = lax.div(group, PER_Q)
        return q, pl.multiple_of(lax.rem(group, PER_Q) * VEC, VEC)

    def load(q):
        return pltpu.make_async_copy(chol_ref.at[q], loaded.at[q], load_sem.at[q])

    def wait_bytes(ref, sem):
        pltpu.make_async_copy(ref, ref, sem).wait()

    barrier = pltpu.get_barrier_semaphore()

    def greet(device):
        pl.semaphore_signal(barrier, inc=1, device_id=device, device_id_type=MESH)

    near_to = (lax.rem(k + 1, 8), core, peer(4))
    near_from = (lax.rem(k + 7, 8), core, peer(4))
    far = (lax.rem(k + 4, 8), core, me)
    for d in range(1, ORB):
        greet((k, 0, peer(d)))

    @pl.when(core == 1)
    def _():
        greet((k, 0, me))
        greet(near_to)
        greet(near_from)
        greet(far)

    for d in range(ORB):
        q, at = place(peer(d) * SLOTS)
        pltpu.make_async_copy(
            chol_ref.at[q, :, :, pl.ds(at, VEC), :], first.at[d], first_sem.at[0]).start()
        q, at = place(peer(d) * SLOTS + WHOLE)
        pltpu.make_async_copy(
            chol_ref.at[q, 1, pl.ds(ALONG - ROWS, 4), pl.ds(at, VEC), :], first_along.at[d],
            first_sem.at[1]).start()

    lane = lax.broadcasted_iota(jnp.int32, (VEC, 128), 1)

    def plane_of(group):
        q, at = place(group)

        def plane(f):
            return pad_lanes(loaded[q, f // ROWS, f % ROWS, pl.ds(at, VEC), :].astype(F32))

        return plane

    def along_of(group):
        q, at = place(group)

        def plane(n):
            return pad_lanes(loaded[q, 1, ALONG - ROWS + n, pl.ds(at, VEC), :].astype(F32))

        return plane

    def fold(plane, put, thin=None):
        for e in range(4):
            riding = plane(KEPT + e)
            for p in range(PIECES):
                f = PIECES * e + p
                moved = pltpu.roll(riding, (NORB - SPARE * p) % 128, 1)
                value = jnp.where(lane < NORB, plane(f), moved)
                if p == PIECES - 1 and thin is not None:
                    value = jnp.where(lane < 128 - THIN, value, thin(e))
                put(f, value)

    def fold_slot(slot, plane, along, put):
        def thin(e):
            number = 4 * slot + e
            which = jnp.where(number < 7, 0, 1)
            piece_at = lax.rem(number, 7)
            return pltpu.roll(along(which), lax.rem(128 + 128 - THIN - THIN * piece_at, 128), 1)

        fold(plane, put, thin)
        for e in range(2):
            f = PIECES * 4 + e
            moved = pltpu.roll(along(2 + e), NORB - SPARE * slot, 1)
            put(f, jnp.where(lane < NORB, plane(f), moved))

    def fold_tail(plane, put):
        riders = [plane(LAST + e) for e in range(4)]
        for e in range(4):
            for p in range(4):
                moved = pltpu.roll(riders[e], (NORB - SPARE * p) % 128, 1)
                put(4 * e + p, jnp.where(lane < NORB, plane(4 * e + p), moved))
        value = plane(16)
        for e in range(3):
            value = jnp.where(lane < NORB + 8 * e, value, pltpu.roll(riders[e], 8 + 8 * e, 1))
        put(16, value)
        put(17, jnp.where(lane < NORB, plane(17), pltpu.roll(riders[3], 8, 1)))

    def halves(put):
        held = {}

        def put_plane(f, value):
            held[f] = value
            if f ^ 1 in held:
                a, b = held[f & ~1], held[f | 1]
                for h in range(2):
                    rows = slice(HALF * h, HALF * h + HALF)
                    put(h, f // 2, jnp.concatenate([a[rows], b[rows]], axis=0).astype(BF16))

        return put_plane

    def send_slot(slot, _, early=False):
        def sources(d):
            if early:
                return (lambda f: pad_lanes(first[d, f // ROWS, f % ROWS].astype(F32)),
                        lambda n: pad_lanes(first_along[d, n].astype(F32)))
            group = peer(d) * SLOTS
            return plane_of(group + slot), along_of(group + WHOLE)

        def send_one(n, _):
            d = ORB - n
            to = peer(d)

            def put(f, value):
                send[slot, d, f] = value.astype(BF16)

            fold_slot(slot, *sources(d), put)
            pltpu.make_async_remote_copy(
                src_ref=send.at[slot, d], dst_ref=recv.at[slot, me], send_sem=pair_send.at[slot],
                recv_sem=pair_recv.at[slot], device_id=(k, core, to), device_id_type=MESH).start()
            return 0

        lax.fori_loop(1, ORB, send_one, 0)

        def put_own(f, value):
            recv[slot, me, f] = value.astype(BF16)

        fold_slot(slot, *sources(0), put_own)
        return 0

    wait_bytes(first, first_sem.at[0])
    wait_bytes(first_along, first_sem.at[1])
    for q in range(2):
        load(q).start()

    @pl.when(core == 0)
    def _():
        pl.semaphore_wait(barrier, 2 * ORB - 1)
        pl.semaphore_signal(ready, inc=1, device_id=(k, 1, me), device_id_type=MESH)

    @pl.when(core == 1)
    def _():
        pl.semaphore_wait(ready, 1)
        for d in range(1, ORB):
            pltpu.make_async_remote_copy(
                src_ref=green_ref, dst_ref=green_mine.at[me], send_sem=gather_send,
                recv_sem=gather_recv, device_id=(k, core, peer(d)), device_id_type=MESH).start()

    send_slot(0, 0, early=True)

    row = lax.broadcasted_iota(jnp.int32, (256, 256), 0)
    col = lax.broadcasted_iota(jnp.int32, (256, 256), 1)
    hit = (lax.div(row, 16) == lax.rem(col, 16)) & (lax.rem(row, 16) == lax.div(col, 16))
    perm[...] = jnp.where(hit, 1.0, 0.0).astype(BF16)
    for at in (PADDED, 128 + PADDED):
        rhs[at:at + 16, :] = jnp.zeros((16, VEC * 256), BF16)
    total[...] = jnp.zeros_like(total)
    weights[...] = jnp.zeros_like(weights)

    for q in range(2):
        load(q).wait()
    send_slot(1, 0)

    @pl.when(core == 1)
    def _():
        green_mine[me] = green_ref[...]
        wait_bytes(green_mine.at[pl.ds(0, ORB - 1)], gather_recv)
        pl.semaphore_wait(barrier, 3)
        for q, device in ((0, near_to), (1, far)):
            pltpu.make_async_remote_copy(
                src_ref=green_mine, dst_ref=green_all.at[q], send_sem=shift_send.at[q],
                recv_sem=shift_recv.at[q], device_id=device, device_id_type=MESH).start()

    lax.fori_loop(2, WHOLE, send_slot, 0)

    for number in range(2):
        plane = plane_of(ORB * SLOTS + number)

        def put_over(h, n, value, number=number):
            send_over[2 * number + h, n] = value

        put = halves(put_over)
        fold(plane, put)
        for f in range(PIECES * 4, KEPT):
            put(f, plane(f))
    for number in range(4):
        to = 2 * number + lax.rem(core + number // 2, 2)

        @pl.when(me != to)
        def _(number=number, to=to):
            pltpu.make_async_remote_copy(
                src_ref=send_over.at[number], dst_ref=recv_over.at[me], send_sem=over_send,
                recv_sem=over_recv, device_id=(k, core, to), device_id_type=MESH).start()

        @pl.when(me == to)
        def _(number=number):
            recv_over[me] = send_over[number]

    def fold_last(d, _):
        def put_last(h, n, value):
            send_last[h, d, n] = value

        fold_tail(plane_of(peer(d) * SLOTS + WHOLE), halves(put_last))
        return 0

    def send_last_half(h):
        def send_one(n, _):
            d = ORB - n
            pltpu.make_async_remote_copy(
                src_ref=send_last.at[h, d], dst_ref=recv_last.at[h, me], send_sem=last_send.at[h],
                recv_sem=last_recv.at[h], device_id=(k, core, peer(d)), device_id_type=MESH).start()
            return 0

        lax.fori_loop(1, ORB, send_one, 0)

    lax.fori_loop(0, ORB, fold_last, 0)
    for h in range(2):
        send_last_half(h)
        recv_last[h, me] = send_last[h, 0]

    hand_green = pltpu.make_async_remote_copy(
        src_ref=green_all, dst_ref=green_all, send_sem=swap_send,
        recv_sem=swap_recv, device_id=(k, 0, me), device_id_type=MESH)

    @pl.when(core == 1)
    def _():
        for q in range(2):
            wait_bytes(green_all.at[q], shift_recv.at[q])
        hand_green.start()

    @pl.when(core == 0)
    def _():
        hand_green.wait_recv()

    for q in range(2):
        for t in range(TAUS):
            parts = []
            for ri in range(2):
                blocks = [green_all[q, o, t, :, ri, :].astype(F32) for o in range(ORB)]
                parts.append(pad_lanes(jnp.concatenate(blocks, axis=0)))
            at = t * 256
            real, imag = parts
            weights[q, 0:NORB, at:at + 128] = real.astype(BF16)
            weights[q, 0:NORB, at + 128:at + 256] = imag.astype(BF16)
            weights[q, 128:128 + NORB, at:at + 128] = (-imag).astype(BF16)
            weights[q, 128:128 + NORB, at + 128:at + 256] = real.astype(BF16)

    swap_half = pltpu.make_async_remote_copy(
        src_ref=total.at[pl.ds(pl.multiple_of(other * half, half), half)], dst_ref=half_in,
        send_sem=half_send, recv_sem=half_recv, device_id=(k, other, me), device_id_type=MESH)

    def pieced(pieces):
        for n, (tile, by, start) in enumerate(pieces):
            back = pltpu.roll(tile.astype(F32), by, 1)
            value = jnp.where(lane >= start, back, value) if n else back
        return value

    def unfold(planes, put):
        for e in range(4):
            put(e, pieced([
                (planes(PIECES * e + p), SPARE + SPARE * p, SPARE * p) for p in range(PIECES)
            ]).astype(BF16))

    def unfold_tail(planes, put):
        for e in range(4):
            pieces = [(planes(4 * e + p), SPARE + SPARE * p, SPARE * p) for p in range(4)]
            pieces.append((planes(16), 120 - 8 * e, 96) if e < 3 else (planes(17), 120, 96))
            put(e, pieced(pieces).astype(BF16))

    def turn(plane, vectors):
        for jb in range(PADDED // 16):
            rows = [j for j in range(16 * jb, 16 * jb + 16) if j < NORB]
            both = jnp.concatenate(
                [jnp.concatenate([plane(j // ROWS, ri * ROWS + j % ROWS) for j in rows], axis=0)
                 for ri in range(2)], axis=1)
            turned = jnp.dot(perm[0:16 * vectors, 0:16 * len(rows)], both,
                             preferred_element_type=F32).astype(BF16)
            for v in range(vectors):
                tile = turned[16 * v:16 * v + 16]
                flat[v, 16 * jb:16 * jb + 16, :] = tile
                rhs[16 * jb:16 * jb + 16, 256 * v:256 * v + 256] = tile
                rhs[128 + 16 * jb:144 + 16 * jb, 256 * v:256 * v + 128] = -tile[:, 128:256]
                rhs[128 + 16 * jb:144 + 16 * jb, 256 * v + 128:256 * v + 256] = tile[:, 0:128]

    def image_of(q, at, vectors):
        step = 4
        for v in range(0, vectors, step):
            left = flat[v:v + step].reshape(step * PADDED, 256)
            for t in range(TAUS):
                y = jnp.dot(left, weights[q, :, 256 * t:256 * t + 256], preferred_element_type=F32)
                for i in range(step):
                    scale = screen_ref[q, t, at + v + i]
                    image[PADDED * t:PADDED * t + PADDED, 256 * (v + i):256 * (v + i) + 256] = (
                        y[PADDED * i:PADDED * i + PADDED] * scale).astype(BF16)

    def add(rows, vectors):
        cols = slice(0, 256 * vectors)
        total[rows] += lax.dot_general(
            image[rows, cols], rhs[:, cols], (((1,), (1,)), ((), ())), preferred_element_type=F32)

    def work_whole(slot, _):
        group = me * SLOTS + slot
        wait_bytes(recv.at[slot, pl.ds(0, ORB - 1)], pair_recv.at[slot])
        for o in range(ORB):
            def put(e, value, o=o):
                extra[o, e] = value

            unfold(lambda f, o=o: recv[slot, o, f], put)
        turn(lambda o, f: recv[slot, o, f] if f < KEPT else extra[o, f - KEPT], VEC)
        image_of(lax.div(group, PER_Q), lax.rem(group, PER_Q) * VEC, VEC)
        add(slice(None), VEC)
        return 0

    def turned_over(value):
        return jnp.concatenate([value[HALF:], value[:HALF]], axis=0)

    def unpack(tiles, kept, spread):
        for o in range(ORB):
            for n in range(kept // 2):
                tile = tiles(o, n)
                bank[o, 2 * n] = tile
                bank[o, 2 * n + 1] = turned_over(tile.astype(F32)).astype(BF16)

            def put(e, value, o=o):
                bank[o, kept + e] = value

            spread(lambda f, o=o: bank[o, f], put)

    def along_planes(o):
        for a in range(2):
            pieces = [divmod(7 * a + m, 4) for m in range(7)]
            yield pieced([(recv[p, o, PIECES * e + 4], THIN + THIN * m, THIN * m)
                          for m, (p, e) in enumerate(pieces)])
        for e in range(2):
            yield pieced([(recv[p, o, 20 + e], SPARE + SPARE * p, SPARE * p) for p in range(WHOLE)])

    def work_half(position, _):
        h = jnp.where(position == 0, lax.rem(over_at, 2), position - 1)
        group = jnp.where(position == 0, ORB * SLOTS + over_at // 2, me * SLOTS + WHOLE)

        @pl.when(position == 0)
        def _():
            wait_bytes(recv_over.at[pl.ds(0, ORB - 1)], over_recv)
            unpack(lambda o, n: recv_over[o, n], KEPT, unfold)

        @pl.when(position != 0)
        def _():
            for o in range(ORB):
                for n, value in enumerate(along_planes(o)):
                    bank[o, ALONG + n] = jnp.where(h == 1, turned_over(value), value).astype(BF16)
            wait_bytes(recv_last.at[h, pl.ds(0, ORB - 1)], last_recv.at[h])
            unpack(lambda o, n: recv_last[h, o, n], LAST, unfold_tail)

        turn(lambda o, f: bank[o, f], HALF)
        image_of(lax.div(group, PER_Q), lax.rem(group, PER_Q) * VEC + HALF * h, HALF)

        @pl.when(position != 2)
        def _():
            add(slice(None), HALF)

        @pl.when(position == 2)
        def _():
            add(pl.ds(pl.multiple_of(other * half, half), half), HALF)
            swap_half.start()
            add(pl.ds(pl.multiple_of(core * half, half), half), HALF)

        return 0

    lax.fori_loop(0, WHOLE, work_whole, 0)
    lax.fori_loop(jnp.where(has_over, 0, 1), 3, work_half, 0)

    swap_half.wait()
    mine[...] = -(total[pl.ds(pl.multiple_of(core * half, half), half), :] + half_in[...])
    for d in (4, 5, 7, 6, 1, 3, 2, 0):
        to = peer(d)
        for t in range(2):
            base = pl.multiple_of(lax.div(ROWS * to, 8) * 8, 8)
            around = mine[pl.ds(t * PADDED + base, 24), :]
            rows = pltpu.roll(around, 24 - (ROWS * to - base), 0)[0:ROWS]
            for ri in range(2):
                at = ROWS * (2 * t + ri)
                cut[d, at:at + ROWS] = rows[:, 128 * ri:128 * ri + 128]
        if d:
            piece[d] = cut[d].astype(BF16)
            pltpu.make_async_remote_copy(
                src_ref=piece.at[d], dst_ref=gathered.at[me], send_sem=piece_send,
                recv_sem=piece_recv, device_id=(k, core, to), device_id_type=MESH).start()
    gathered[me] = jnp.zeros_like(piece[0])
    wait_bytes(gathered.at[pl.ds(0, ORB - 1)], piece_recv)
    summed = cut[0]
    for o in range(ORB):
        summed = summed + gathered[o].astype(F32)
    result[...] = summed
    hand_over = pltpu.make_async_remote_copy(
        src_ref=result, dst_ref=result_in, send_sem=out_send, recv_sem=out_recv,
        device_id=(k, other, me), device_id_type=MESH)
    hand_over.start()

    def put_out(which, ref):
        for t in range(2):
            for ri in range(2):
                at = ROWS * (2 * t + ri)
                out_ref[2 * which + t, :, ri, :] = ref[at:at + ROWS, 0:NORB]

    put_out(core, result)

    wait_bytes(piece.at[pl.ds(0, ORB - 1)], piece_send)

    def sent_slot(slot, _):
        wait_bytes(recv.at[slot, pl.ds(0, ORB - 1)], pair_send.at[slot])
        return 0

    lax.fori_loop(0, WHOLE, sent_slot, 0)
    for h in range(2):
        wait_bytes(recv_last.at[h, pl.ds(0, ORB - 1)], last_send.at[h])

    @pl.when(has_over)
    def _():
        wait_bytes(recv_over.at[pl.ds(0, 3)], over_send)

    @pl.when(jnp.logical_not(has_over))
    def _():
        wait_bytes(recv_over.at[pl.ds(0, 4)], over_send)

    @pl.when(core == 1)
    def _():
        wait_bytes(green_mine.at[pl.ds(0, ORB - 1)], gather_send)
        for q in range(2):
            wait_bytes(green_mine, shift_send.at[q])
        hand_green.wait_send()

    hand_over.wait()
    put_out(other, result_in)


def body(chol_pairs, green, screening):
    planes = jnp.transpose(chol_pairs[:, 0], (0, 1, 3, 2, 4))
    dma = pltpu.SemaphoreType.DMA
    out = pl.pallas_call(
        kernel,
        out_shape=pltpu.VMEM((TAUS, ROWS, 2, NORB), F32),
        in_specs=[
            pl.BlockSpec(memory_space=pl.ANY),
            pl.BlockSpec(memory_space=pltpu.VMEM),
            pl.BlockSpec(memory_space=pltpu.SMEM),
        ],
        out_specs=pl.BlockSpec(memory_space=pltpu.VMEM),
        scratch_shapes=[
            pltpu.VMEM((2, 2, ROWS, PER_Q * VEC, NORB), BF16),
            pltpu.VMEM((ORB, 2, ROWS, VEC, NORB), BF16),
            pltpu.VMEM((ORB, 4, VEC, NORB), BF16),
            pltpu.VMEM((WHOLE, ORB, KEPT, VEC, 128), BF16),
            pltpu.VMEM((2, ORB, LAST // 2, VEC, 128), BF16),
            pltpu.VMEM((4, KEPT // 2, VEC, 128), BF16),
            pltpu.VMEM((WHOLE, ORB, KEPT, VEC, 128), BF16),
            pltpu.VMEM((2, ORB, LAST // 2, VEC, 128), BF16),
            pltpu.VMEM((ORB, KEPT // 2, VEC, 128), BF16),
            pltpu.VMEM((ORB, PLANES, VEC, 128), BF16),
            pltpu.VMEM((ORB, PLANES - KEPT, VEC, 128), BF16),
            pltpu.VMEM((VEC, PADDED, 256), BF16),
            pltpu.VMEM((TAUS * PADDED, VEC * 256), BF16),
            pltpu.VMEM((256, VEC * 256), BF16),
            pltpu.VMEM((2, 256, TAUS * 256), BF16),
            pltpu.VMEM((256, 256), BF16),
            pltpu.VMEM((TAUS * PADDED, 256), F32),
            pltpu.VMEM((2 * PADDED, 256), F32),
            pltpu.VMEM((ORB, TAUS, ROWS, 2, NORB), BF16),
            pltpu.VMEM((2, ORB, TAUS, ROWS, 2, NORB), BF16),
            pltpu.VMEM((2 * PADDED, 256), F32),
            pltpu.VMEM((ORB, 64, 128), F32),
            pltpu.VMEM((ORB, 64, 128), BF16),
            pltpu.VMEM((ORB, 64, 128), BF16),
            pltpu.VMEM((64, 128), F32),
            pltpu.VMEM((64, 128), F32),
            dma((2,)), dma((2,)), pltpu.SemaphoreType.REGULAR, dma, dma, dma((2,)), dma((2,)), dma, dma,
            dma((WHOLE,)), dma((WHOLE,)), dma((2,)), dma((2,)), dma, dma,
            dma, dma, dma, dma, dma, dma,
        ],
        compiler_params=pltpu.CompilerParams(
            collective_id=0, has_side_effects=True, vmem_limit_bytes=56 * 1024 * 1024),
        cost_estimate=pl.CostEstimate(
            flops=7_200_000_000, bytes_accessed=5_400_000, transcendentals=0),
    )(planes, jnp.transpose(green[0], (0, 2, 1, 3)), screening)
    return jnp.transpose(out, (0, 2, 1, 3))[None]


def solution(mesh):
    placed = (
        P(None, "ka", None, "chol", "orb", None),
        P("ka", None, None, "orb", None),
        P(None, None, "chol"),
    )
    return jax.shard_map(
        body,
        mesh=mesh,
        in_specs=placed,
        out_specs=P("ka", None, None, "orb", None),
        check_vma=False,
    )
```

```python
import functools

import jax
import jax.numpy as jnp
from jax import lax
from jax.experimental import pallas as pl
from jax.experimental.pallas import tpu as pltpu
from jax.sharding import PartitionSpec as P

MESH = pl.DeviceIdType.MESH
BF16 = jnp.bfloat16
F32 = jnp.float32

ORB = 8
ROWS = 13
NORB = 104
PADDED = 112
TAUS = 4
VEC = 16
PER_Q = 25
SLOTS = 6
WHOLE = SLOTS - 1
HALF = VEC // 2
PLANES = 2 * ROWS
KEPT = 22
LAST = 18
ALONG = LAST + 4
THIN = 16
SPARE = 128 - NORB
PIECES = 5


def pad_lanes(x):
    return jnp.concatenate([x, jnp.zeros((x.shape[0], 128 - x.shape[1]), x.dtype)], axis=1)


def kernel(
    chol_ref, green_ref, screen_ref, out_ref,
    loaded, first, first_along, send, send_last, send_over, recv, recv_last, recv_over, bank, extra, flat, image, rhs, weights, perm, total,
    green_mine, green_all, half_in, cut, piece, gathered, result, result_in,
    load_sem, first_sem, ready, gather_send, gather_recv, shift_send, shift_recv, swap_send, swap_recv,
    pair_send, pair_recv, last_send, last_recv, over_send, over_recv, half_send, half_recv, piece_send, piece_recv, out_send, out_recv,
):
    k = lax.axis_index("ka")
    core = lax.axis_index("chol")
    me = lax.axis_index("orb")
    other = 1 - core
    has_over = lax.rem(me // 4 + lax.rem(me, 4), 2) == core
    over_at = me // 2
    half = 2 * PADDED

    def peer(d):
        dx, dy = d // 4, d % 4
        x = lax.rem(me // 4 + dx, 2)
        y = lax.rem(lax.rem(me, 4) + dy, 4)
        return x * 4 + y

    def place(group):
        q = lax.div(group, PER_Q)
        return q, pl.multiple_of(lax.rem(group, PER_Q) * VEC, VEC)

    def load(q):
        return pltpu.make_async_copy(chol_ref.at[q], loaded.at[q], load_sem.at[q])

    def wait_bytes(ref, sem):
        pltpu.make_async_copy(ref, ref, sem).wait()

    barrier = pltpu.get_barrier_semaphore()

    def greet(device):
        pl.semaphore_signal(barrier, inc=1, device_id=device, device_id_type=MESH)

    near_to = (lax.rem(k + 1, 8), core, peer(4))
    near_from = (lax.rem(k + 7, 8), core, peer(4))
    far = (lax.rem(k + 4, 8), core, me)
    for d in range(1, ORB):
        greet((k, 0, peer(d)))

    @pl.when(core == 1)
    def _():
        greet((k, 0, me))
        greet(near_to)
        greet(near_from)
        greet(far)

    for d in range(ORB):
        q, at = place(peer(d) * SLOTS)
        pltpu.make_async_copy(
            chol_ref.at[q, :, :, pl.ds(at, VEC), :], first.at[d], first_sem.at[0]).start()
        q, at = place(peer(d) * SLOTS + WHOLE)
        pltpu.make_async_copy(
            chol_ref.at[q, 1, pl.ds(ALONG - ROWS, 4), pl.ds(at, VEC), :], first_along.at[d],
            first_sem.at[1]).start()

    lane = lax.broadcasted_iota(jnp.int32, (VEC, 128), 1)

    def plane_of(group):
        q, at = place(group)

        def plane(f):
            return pad_lanes(loaded[q, f // ROWS, f % ROWS, pl.ds(at, VEC), :].astype(F32))

        return plane

    def along_of(group):
        q, at = place(group)

        def plane(n):
            return pad_lanes(loaded[q, 1, ALONG - ROWS + n, pl.ds(at, VEC), :].astype(F32))

        return plane

    def fold(plane, put, thin=None):
        for e in range(4):
            riding = plane(KEPT + e)
            for p in range(PIECES):
                f = PIECES * e + p
                moved = pltpu.roll(riding, (NORB - SPARE * p) % 128, 1)
                value = jnp.where(lane < NORB, plane(f), moved)
                if p == PIECES - 1 and thin is not None:
                    value = jnp.where(lane < 128 - THIN, value, thin(e))
                put(f, value)

    def fold_slot(slot, plane, along, put):
        def thin(e):
            number = 4 * slot + e
            which = jnp.where(number < 7, 0, 1)
            piece_at = lax.rem(number, 7)
            return pltpu.roll(along(which), lax.rem(128 + 128 - THIN - THIN * piece_at, 128), 1)

        fold(plane, put, thin)
        for e in range(2):
            f = PIECES * 4 + e
            moved = pltpu.roll(along(2 + e), NORB - SPARE * slot, 1)
            put(f, jnp.where(lane < NORB, plane(f), moved))

    def fold_tail(plane, put):
        riders = [plane(LAST + e) for e in range(4)]
        for e in range(4):
            for p in range(4):
                moved = pltpu.roll(riders[e], (NORB - SPARE * p) % 128, 1)
                put(4 * e + p, jnp.where(lane < NORB, plane(4 * e + p), moved))
        value = plane(16)
        for e in range(3):
            value = jnp.where(lane < NORB + 8 * e, value, pltpu.roll(riders[e], 8 + 8 * e, 1))
        put(16, value)
        put(17, jnp.where(lane < NORB, plane(17), pltpu.roll(riders[3], 8, 1)))

    def halves(put):
        held = {}

        def put_plane(f, value):
            held[f] = value
            if f ^ 1 in held:
                a, b = held[f & ~1], held[f | 1]
                for h in range(2):
                    rows = slice(HALF * h, HALF * h + HALF)
                    put(h, f // 2, jnp.concatenate([a[rows], b[rows]], axis=0).astype(BF16))

        return put_plane

    def send_slot(slot, _, early=False):
        def sources(d):
            if early:
                return (lambda f: pad_lanes(first[d, f // ROWS, f % ROWS].astype(F32)),
                        lambda n: pad_lanes(first_along[d, n].astype(F32)))
            group = peer(d) * SLOTS
            return plane_of(group + slot), along_of(group + WHOLE)

        def send_one(n, _):
            d = ORB - n
            to = peer(d)

            def put(f, value):
                send[slot, d, f] = value.astype(BF16)

            fold_slot(slot, *sources(d), put)
            pltpu.make_async_remote_copy(
                src_ref=send.at[slot, d], dst_ref=recv.at[slot, me], send_sem=pair_send.at[slot],
                recv_sem=pair_recv.at[slot], device_id=(k, core, to), device_id_type=MESH).start()
            return 0

        lax.fori_loop(1, ORB, send_one, 0)

        def put_own(f, value):
            recv[slot, me, f] = value.astype(BF16)

        fold_slot(slot, *sources(0), put_own)
        return 0

    wait_bytes(first, first_sem.at[0])
    wait_bytes(first_along, first_sem.at[1])
    for q in range(2):
        load(q).start()

    @pl.when(core == 0)
    def _():
        pl.semaphore_wait(barrier, 2 * ORB - 1)
        pl.semaphore_signal(ready, inc=1, device_id=(k, 1, me), device_id_type=MESH)

    @pl.when(core == 1)
    def _():
        pl.semaphore_wait(ready, 1)
        for d in range(1, ORB):
            pltpu.make_async_remote_copy(
                src_ref=green_ref, dst_ref=green_mine.at[me], send_sem=gather_send,
                recv_sem=gather_recv, device_id=(k, core, peer(d)), device_id_type=MESH).start()

    send_slot(0, 0, early=True)

    row = lax.broadcasted_iota(jnp.int32, (256, 256), 0)
    col = lax.broadcasted_iota(jnp.int32, (256, 256), 1)
    hit = (lax.div(row, 16) == lax.rem(col, 16)) & (lax.rem(row, 16) == lax.div(col, 16))
    perm[...] = jnp.where(hit, 1.0, 0.0).astype(BF16)
    for at in (PADDED, 128 + PADDED):
        rhs[at:at + 16, :] = jnp.zeros((16, VEC * 256), BF16)
    total[...] = jnp.zeros_like(total)
    weights[...] = jnp.zeros_like(weights)

    for q in range(2):
        load(q).wait()
    send_slot(1, 0)

    @pl.when(core == 1)
    def _():
        green_mine[me] = green_ref[...]
        wait_bytes(green_mine.at[pl.ds(0, ORB - 1)], gather_recv)
        pl.semaphore_wait(barrier, 3)
        for q, device in ((0, near_to), (1, far)):
            pltpu.make_async_remote_copy(
                src_ref=green_mine, dst_ref=green_all.at[q], send_sem=shift_send.at[q],
                recv_sem=shift_recv.at[q], device_id=device, device_id_type=MESH).start()

    lax.fori_loop(2, WHOLE, send_slot, 0)

    for number in range(2):
        plane = plane_of(ORB * SLOTS + number)

        def put_over(h, n, value, number=number):
            send_over[2 * number + h, n] = value

        put = halves(put_over)
        fold(plane, put)
        for f in range(PIECES * 4, KEPT):
            put(f, plane(f))
    for number in range(4):
        to = 2 * number + lax.rem(core + number // 2, 2)

        @pl.when(me != to)
        def _(number=number, to=to):
            pltpu.make_async_remote_copy(
                src_ref=send_over.at[number], dst_ref=recv_over.at[me], send_sem=over_send,
                recv_sem=over_recv, device_id=(k, core, to), device_id_type=MESH).start()

        @pl.when(me == to)
        def _(number=number):
            recv_over[me] = send_over[number]

    def fold_last(d, _):
        def put_last(h, n, value):
            send_last[h, d, n] = value

        fold_tail(plane_of(peer(d) * SLOTS + WHOLE), halves(put_last))
        return 0

    def send_last_half(h):
        def send_one(n, _):
            d = ORB - n
            pltpu.make_async_remote_copy(
                src_ref=send_last.at[h, d], dst_ref=recv_last.at[h, me], send_sem=last_send.at[h],
                recv_sem=last_recv.at[h], device_id=(k, core, peer(d)), device_id_type=MESH).start()
            return 0

        lax.fori_loop(1, ORB, send_one, 0)

    lax.fori_loop(0, ORB, fold_last, 0)
    for h in range(2):
        send_last_half(h)
        recv_last[h, me] = send_last[h, 0]

    hand_green = pltpu.make_async_remote_copy(
        src_ref=green_all, dst_ref=green_all, send_sem=swap_send,
        recv_sem=swap_recv, device_id=(k, 0, me), device_id_type=MESH)

    @pl.when(core == 1)
    def _():
        for q in range(2):
            wait_bytes(green_all.at[q], shift_recv.at[q])
        hand_green.start()

    @pl.when(core == 0)
    def _():
        hand_green.wait_recv()

    for q in range(2):
        for t in range(TAUS):
            parts = []
            for ri in range(2):
                blocks = [green_all[q, o, t, :, ri, :].astype(F32) for o in range(ORB)]
                parts.append(pad_lanes(jnp.concatenate(blocks, axis=0)))
            at = t * 256
            real, imag = parts
            weights[q, 0:NORB, at:at + 128] = real.astype(BF16)
            weights[q, 0:NORB, at + 128:at + 256] = imag.astype(BF16)
            weights[q, 128:128 + NORB, at:at + 128] = (-imag).astype(BF16)
            weights[q, 128:128 + NORB, at + 128:at + 256] = real.astype(BF16)

    swap_half = pltpu.make_async_remote_copy(
        src_ref=total.at[pl.ds(pl.multiple_of(other * half, half), half)], dst_ref=half_in,
        send_sem=half_send, recv_sem=half_recv, device_id=(k, other, me), device_id_type=MESH)

    def pieced(pieces):
        for n, (tile, by, start) in enumerate(pieces):
            back = pltpu.roll(tile.astype(F32), by, 1)
            value = jnp.where(lane >= start, back, value) if n else back
        return value

    def unfold(planes, put):
        for e in range(4):
            put(e, pieced([
                (planes(PIECES * e + p), SPARE + SPARE * p, SPARE * p) for p in range(PIECES)
            ]).astype(BF16))

    def unfold_tail(planes, put):
        for e in range(4):
            pieces = [(planes(4 * e + p), SPARE + SPARE * p, SPARE * p) for p in range(4)]
            pieces.append((planes(16), 120 - 8 * e, 96) if e < 3 else (planes(17), 120, 96))
            put(e, pieced(pieces).astype(BF16))

    def turn(plane, vectors):
        for jb in range(PADDED // 16):
            rows = [j for j in range(16 * jb, 16 * jb + 16) if j < NORB]
            both = jnp.concatenate(
                [jnp.concatenate([plane(j // ROWS, ri * ROWS + j % ROWS) for j in rows], axis=0)
                 for ri in range(2)], axis=1)
            turned = jnp.dot(perm[0:16 * vectors, 0:16 * len(rows)], both,
                             preferred_element_type=F32).astype(BF16)
            for v in range(vectors):
                tile = turned[16 * v:16 * v + 16]
                flat[v, 16 * jb:16 * jb + 16, :] = tile
                rhs[16 * jb:16 * jb + 16, 256 * v:256 * v + 256] = tile
                rhs[128 + 16 * jb:144 + 16 * jb, 256 * v:256 * v + 128] = -tile[:, 128:256]
                rhs[128 + 16 * jb:144 + 16 * jb, 256 * v + 128:256 * v + 256] = tile[:, 0:128]

    def image_of(q, at, vectors):
        step = 4
        for v in range(0, vectors, step):
            left = flat[v:v + step].reshape(step * PADDED, 256)
            for t in range(TAUS):
                y = jnp.dot(left, weights[q, :, 256 * t:256 * t + 256], preferred_element_type=F32)
                for i in range(step):
                    scale = screen_ref[q, t, at + v + i]
                    image[PADDED * t:PADDED * t + PADDED, 256 * (v + i):256 * (v + i) + 256] = (
                        y[PADDED * i:PADDED * i + PADDED] * scale).astype(BF16)

    def add(rows, vectors):
        cols = slice(0, 256 * vectors)
        total[rows] += lax.dot_general(
            image[rows, cols], rhs[:, cols], (((1,), (1,)), ((), ())), preferred_element_type=F32)

    def work_whole(slot, _):
        group = me * SLOTS + slot
        wait_bytes(recv.at[slot, pl.ds(0, ORB - 1)], pair_recv.at[slot])
        for o in range(ORB):
            def put(e, value, o=o):
                extra[o, e] = value

            unfold(lambda f, o=o: recv[slot, o, f], put)
        turn(lambda o, f: recv[slot, o, f] if f < KEPT else extra[o, f - KEPT], VEC)
        image_of(lax.div(group, PER_Q), lax.rem(group, PER_Q) * VEC, VEC)
        add(slice(None), VEC)
        return 0

    def turned_over(value):
        return jnp.concatenate([value[HALF:], value[:HALF]], axis=0)

    def unpack(tiles, kept, spread):
        for o in range(ORB):
            for n in range(kept // 2):
                tile = tiles(o, n)
                bank[o, 2 * n] = tile
                bank[o, 2 * n + 1] = turned_over(tile.astype(F32)).astype(BF16)

            def put(e, value, o=o):
                bank[o, kept + e] = value

            spread(lambda f, o=o: bank[o, f], put)

    def along_planes(o):
        for a in range(2):
            pieces = [divmod(7 * a + m, 4) for m in range(7)]
            yield pieced([(recv[p, o, PIECES * e + 4], THIN + THIN * m, THIN * m)
                          for m, (p, e) in enumerate(pieces)])
        for e in range(2):
            yield pieced([(recv[p, o, 20 + e], SPARE + SPARE * p, SPARE * p) for p in range(WHOLE)])

    def work_half(position, _):
        h = jnp.where(position == 0, lax.rem(over_at, 2), position - 1)
        group = jnp.where(position == 0, ORB * SLOTS + over_at // 2, me * SLOTS + WHOLE)

        @pl.when(position == 0)
        def _():
            wait_bytes(recv_over.at[pl.ds(0, ORB - 1)], over_recv)
            unpack(lambda o, n: recv_over[o, n], KEPT, unfold)

        @pl.when(position != 0)
        def _():
            for o in range(ORB):
                for n, value in enumerate(along_planes(o)):
                    bank[o, ALONG + n] = jnp.where(h == 1, turned_over(value), value).astype(BF16)
            wait_bytes(recv_last.at[h, pl.ds(0, ORB - 1)], last_recv.at[h])
            unpack(lambda o, n: recv_last[h, o, n], LAST, unfold_tail)

        turn(lambda o, f: bank[o, f], HALF)
        image_of(lax.div(group, PER_Q), lax.rem(group, PER_Q) * VEC + HALF * h, HALF)

        @pl.when(position != 2)
        def _():
            add(slice(None), HALF)

        @pl.when(position == 2)
        def _():
            add(pl.ds(pl.multiple_of(other * half, half), half), HALF)
            swap_half.start()
            add(pl.ds(pl.multiple_of(core * half, half), half), HALF)

        return 0

    lax.fori_loop(0, WHOLE, work_whole, 0)
    lax.fori_loop(jnp.where(has_over, 0, 1), 3, work_half, 0)

    swap_half.wait_recv()
    for d in (4, 5, 7, 6, 1, 3, 2, 0):
        to = peer(d)
        for t in range(2):
            base = pl.multiple_of(lax.div(ROWS * to, 8) * 8, 8)
            here = pl.multiple_of(core * half + t * PADDED + base, 8)
            around = total[pl.ds(here, 24), :] + half_in[pl.ds(t * PADDED + base, 24), :]
            rows = -pltpu.roll(around, 24 - (ROWS * to - base), 0)[0:ROWS]
            for ri in range(2):
                at = ROWS * (2 * t + ri)
                cut[d, at:at + ROWS] = rows[:, 128 * ri:128 * ri + 128]
        if d:
            piece[d] = cut[d].astype(BF16)
            pltpu.make_async_remote_copy(
                src_ref=piece.at[d], dst_ref=gathered.at[me], send_sem=piece_send,
                recv_sem=piece_recv, device_id=(k, core, to), device_id_type=MESH).start()
    gathered[me] = jnp.zeros_like(piece[0])
    wait_bytes(gathered.at[pl.ds(0, ORB - 1)], piece_recv)
    summed = cut[0]
    for o in range(ORB):
        summed = summed + gathered[o].astype(F32)
    result[...] = summed
    hand_over = pltpu.make_async_remote_copy(
        src_ref=result, dst_ref=result_in, send_sem=out_send, recv_sem=out_recv,
        device_id=(k, other, me), device_id_type=MESH)
    hand_over.start()

    def put_out(which, ref):
        for t in range(2):
            for ri in range(2):
                at = ROWS * (2 * t + ri)
                out_ref[2 * which + t, :, ri, :] = ref[at:at + ROWS, 0:NORB]

    put_out(core, result)

    swap_half.wait_send()
    wait_bytes(piece.at[pl.ds(0, ORB - 1)], piece_send)

    def sent_slot(slot, _):
        wait_bytes(recv.at[slot, pl.ds(0, ORB - 1)], pair_send.at[slot])
        return 0

    lax.fori_loop(0, WHOLE, sent_slot, 0)
    for h in range(2):
        wait_bytes(recv_last.at[h, pl.ds(0, ORB - 1)], last_send.at[h])

    @pl.when(has_over)
    def _():
        wait_bytes(recv_over.at[pl.ds(0, 3)], over_send)

    @pl.when(jnp.logical_not(has_over))
    def _():
        wait_bytes(recv_over.at[pl.ds(0, 4)], over_send)

    @pl.when(core == 1)
    def _():
        wait_bytes(green_mine.at[pl.ds(0, ORB - 1)], gather_send)
        for q in range(2):
            wait_bytes(green_mine, shift_send.at[q])
        hand_green.wait_send()

    hand_over.wait()
    put_out(other, result_in)


def body(chol_pairs, green, screening):
    planes = jnp.transpose(chol_pairs[:, 0], (0, 1, 3, 2, 4))
    dma = pltpu.SemaphoreType.DMA
    out = pl.pallas_call(
        kernel,
        out_shape=pltpu.VMEM((TAUS, ROWS, 2, NORB), F32),
        in_specs=[
            pl.BlockSpec(memory_space=pl.ANY),
            pl.BlockSpec(memory_space=pltpu.VMEM),
            pl.BlockSpec(memory_space=pltpu.SMEM),
        ],
        out_specs=pl.BlockSpec(memory_space=pltpu.VMEM),
        scratch_shapes=[
            pltpu.VMEM((2, 2, ROWS, PER_Q * VEC, NORB), BF16),
            pltpu.VMEM((ORB, 2, ROWS, VEC, NORB), BF16),
            pltpu.VMEM((ORB, 4, VEC, NORB), BF16),
            pltpu.VMEM((WHOLE, ORB, KEPT, VEC, 128), BF16),
            pltpu.VMEM((2, ORB, LAST // 2, VEC, 128), BF16),
            pltpu.VMEM((4, KEPT // 2, VEC, 128), BF16),
            pltpu.VMEM((WHOLE, ORB, KEPT, VEC, 128), BF16),
            pltpu.VMEM((2, ORB, LAST // 2, VEC, 128), BF16),
            pltpu.VMEM((ORB, KEPT // 2, VEC, 128), BF16),
            pltpu.VMEM((ORB, PLANES, VEC, 128), BF16),
            pltpu.VMEM((ORB, PLANES - KEPT, VEC, 128), BF16),
            pltpu.VMEM((VEC, PADDED, 256), BF16),
            pltpu.VMEM((TAUS * PADDED, VEC * 256), BF16),
            pltpu.VMEM((256, VEC * 256), BF16),
            pltpu.VMEM((2, 256, TAUS * 256), BF16),
            pltpu.VMEM((256, 256), BF16),
            pltpu.VMEM((TAUS * PADDED, 256), F32),
            pltpu.VMEM((ORB, TAUS, ROWS, 2, NORB), BF16),
            pltpu.VMEM((2, ORB, TAUS, ROWS, 2, NORB), BF16),
            pltpu.VMEM((2 * PADDED, 256), F32),
            pltpu.VMEM((ORB, 64, 128), F32),
            pltpu.VMEM((ORB, 64, 128), BF16),
            pltpu.VMEM((ORB, 64, 128), BF16),
            pltpu.VMEM((64, 128), F32),
            pltpu.VMEM((64, 128), F32),
            dma((2,)), dma((2,)), pltpu.SemaphoreType.REGULAR, dma, dma, dma((2,)), dma((2,)), dma, dma,
            dma((WHOLE,)), dma((WHOLE,)), dma((2,)), dma((2,)), dma, dma,
            dma, dma, dma, dma, dma, dma,
        ],
        compiler_params=pltpu.CompilerParams(
            collective_id=0, has_side_effects=True, vmem_limit_bytes=56 * 1024 * 1024),
        cost_estimate=pl.CostEstimate(
            flops=7_200_000_000, bytes_accessed=5_400_000, transcendentals=0),
    )(planes, jnp.transpose(green[0], (0, 2, 1, 3)), screening)
    return jnp.transpose(out, (0, 2, 1, 3))[None]


def solution(mesh):
    placed = (
        P(None, "ka", None, "chol", "orb", None),
        P("ka", None, None, "orb", None),
        P(None, None, "chol"),
    )
    return jax.shard_map(
        body,
        mesh=mesh,
        in_specs=placed,
        out_specs=P("ka", None, None, "orb", None),
        check_vma=False,
    )
```
